256 devices in a mesh: seq: 64 (over z, y, core), head: 4 (over x).
Axes of the slice: x: 4, y: 4, z: 8, core: 2. Of those that a mesh axis runs over, the one named last changes fastest.
Arguments:
- queries: bfloat16 [65536, 5120], P('seq', 'head'), may hold values from -96 to 96
- keys: bfloat16 [65536, 5120], P('seq', 'head'), may hold values from -4.5 to 4.5
- values: bfloat16 [65536, 5120], P('seq', 'head'), may hold values from -6 to 6
- head_class: int32 [40], P('head'), may hold values from 0 to 1, as said below
- mask_spatial: int32 [64, 8, 8], P('seq'), may hold values from 0 to 1, as said below
- mask_temporal: int32 [256, 2, 2], P('seq'), may hold values from 0 to 1, as said below
Outputs:
- attended: bfloat16 [65536, 5120], P('seq', 'head')
The draws below stay inside these ranges and needn't reach their ends.
Inputs may be any that keep to these rules, and one draw needn't show every extreme that they name: `head_class`: each aligned block of 10 heads holds exactly 4 temporal heads. `mask_spatial`: every diagonal tile is 1. `mask_temporal`: every diagonal tile is 1.
All inputs are finite; a program needn't handle non-finite values.
Results may differ from the reference program's by a relative error of at most 0.0044.
Values may be sent and summed in bfloat16 or wider, within the bound.
A program may use at most 128 MiB of HBM per device.

```python
import jax
import jax.numpy as jnp
from jax import lax

HEADS = 40
HEAD_DIM = 128
POSITIONS = 1024
HT_DEV = 4
H_DEV = 10
FRAMES = 64
TOKENS = 65536
GROUPS = 256
GROUP = 4
TILES_S = 8
TILES_T = 2


def shared_rows(key):
    base = jax.random.normal(jax.random.fold_in(key, 11), (TOKENS, HEADS, HEAD_DIM), jnp.float32)
    return jnp.clip(base, -4.5, 4.5)


def draw_keys(key, part):
    base = shared_rows(key)
    return base.reshape(TOKENS, HEADS * HEAD_DIM).astype(jnp.bfloat16)


def draw_queries(key, part):
    key = jax.random.fold_in(key, 2)
    result = jnp.clip(jax.random.normal(jax.random.fold_in(key, 3), (TOKENS, HEADS, HEAD_DIM), jnp.float32), -6.0, 6.0)
    return result.reshape(TOKENS, HEADS * HEAD_DIM).astype(jnp.bfloat16)


def draw_head_class(key, part):
    key = jax.random.fold_in(key, 6)
    blocks = HEADS // H_DEV
    scores = jax.random.randint(key, (blocks, H_DEV), 0, 1 << 20) * H_DEV + jnp.arange(H_DEV, dtype=jnp.int32)[None, :]
    ranks = jnp.argsort(jnp.argsort(scores, axis=1), axis=1)
    return (ranks < HT_DEV).astype(jnp.int32).reshape(HEADS)


def tile_mask(key, count, tiles):
    level = jax.random.randint(jax.random.fold_in(key, 1), (count, 1, 1), 1, 5)
    bits = jax.random.randint(jax.random.fold_in(key, 2), (count, tiles, tiles), 0, 16) < level
    eye = jnp.eye(tiles, dtype=jnp.int32)[None] > 0
    return jnp.logical_or(bits, eye).astype(jnp.int32)


def draw_mask_spatial(key, part):
    key = jax.random.fold_in(key, 7)
    return tile_mask(key, FRAMES, TILES_S)


def draw_mask_temporal(key, part):
    key = jax.random.fold_in(key, 8)
    return tile_mask(key, GROUPS, TILES_T)


def block_scale(own_key, dims, cuts, low, largest):
    def one(axis_at, parts):
        draws = jax.random.uniform(jax.random.fold_in(jax.random.fold_in(own_key, 6), axis_at), (parts,), jnp.float32, low / len(cuts), largest / len(cuts))
        return jnp.repeat(jnp.exp(draws), dims[axis_at] // parts).reshape((-1,) + (1,) * (len(dims) - axis_at - 1))

    factor_of = one(*cuts[0])
    for cut in cuts[1:]:
        factor_of = factor_of * one(*cut)
    return factor_of


def bell_draw(rng, shape, deviation, most, shards=(), kind=jnp.bfloat16):
    entries = deviation * jax.random.normal(rng, shape, jnp.float32)
    if shards:
        entries = entries * block_scale(rng, shape, shards, -0.22, 0.18)
    return jnp.clip(entries, -most, most).astype(kind)


def setup_inputs(seed: int = 0) -> dict:
    key_list = jax.random.split(jax.random.key(seed), 7)
    return {
        "queries": draw_queries(jax.random.fold_in(key_list[6], 71), 0),
        "keys": draw_keys(jax.random.fold_in(key_list[6], 71), 0),
        "values": bell_draw(key_list[2], (TOKENS, HEADS * HEAD_DIM), 1.0, 6.0, ((0, 64), (1, 4))),
        "head_class": draw_head_class(jax.random.fold_in(key_list[6], 71), 0),
        "mask_spatial": draw_mask_spatial(jax.random.fold_in(key_list[6], 71), 0),
        "mask_temporal": draw_mask_temporal(jax.random.fold_in(key_list[6], 71), 0),
    }


def widen_mask(mask):
    allowed = mask > 0
    return jnp.repeat(jnp.repeat(allowed, 128, axis=1), 128, axis=2)


def attend(query, key_rows, value_rows, allowed):
    qf = query.astype(jnp.float32)
    kf = key_rows.astype(jnp.float32)
    vf = value_rows.astype(jnp.float32)
    scores = jnp.einsum('bqhd,bkhd->bhqk', qf, kf) * (query.shape[-1] ** -0.5)
    scores = jnp.where(allowed[:, None], scores, -1e30)
    top = jnp.max(scores, axis=-1, keepdims=True)
    weights = jnp.exp(scores - top)
    total = jnp.sum(weights, axis=-1, keepdims=True)
    low = lax.optimization_barrier(weights.astype(jnp.bfloat16))
    mixed = jnp.einsum('bhqk,bkhd->bhqd', low.astype(jnp.float32), vf) / total
    return jnp.transpose(mixed, (0, 2, 1, 3)).astype(jnp.bfloat16)


def reference(queries, keys, values, head_class, mask_spatial, mask_temporal):
    def split_heads(array):
        return jnp.transpose(array.reshape(FRAMES, POSITIONS, HEADS, HEAD_DIM), (2, 0, 1, 3))

    spatial_allowed = widen_mask(mask_spatial)
    temporal_allowed = widen_mask(mask_temporal)

    def spatial(qh, kh, vh):
        out = attend(qh[:, :, None], kh[:, :, None], vh[:, :, None], spatial_allowed)
        return out[:, :, 0]

    def regroup(array):
        grouped = array.reshape(FRAMES, GROUPS, GROUP, HEAD_DIM)
        return jnp.transpose(grouped, (1, 2, 0, 3)).reshape(GROUPS, GROUP * FRAMES, 1, HEAD_DIM)

    def temporal(qh, kh, vh):
        out = attend(regroup(qh), regroup(kh), regroup(vh), temporal_allowed)
        out = out.reshape(GROUPS, GROUP, FRAMES, HEAD_DIM)
        return jnp.transpose(out, (2, 0, 1, 3)).reshape(FRAMES, POSITIONS, HEAD_DIM)

    def one_head(items):
        qh, kh, vh, kind = items
        return lax.cond(kind > 0, temporal, spatial, qh, kh, vh)

    stacked = lax.map(one_head, (split_heads(queries), split_heads(keys), split_heads(values), head_class))
    return jnp.transpose(stacked, (1, 2, 0, 3)).reshape(TOKENS, HEADS * HEAD_DIM)
```

```python
import functools
import math

import jax
import jax.numpy as jnp
from jax import lax
from jax.experimental import pallas as pl
from jax.experimental.pallas import tpu as pltpu
from jax.sharding import PartitionSpec as P

HEAD_DIM = 128
TILE = 128
LOCAL_HEADS = 10
HT_DEV = 4
HS_DEV = LOCAL_HEADS - HT_DEV
ROWS = 1024
SEQ = 64
PIECE = ROWS // SEQ
NZ, NY, NC = 8, 4, 2
STEP = 256
EXP_SCALE = HEAD_DIM**-0.5 * math.log2(math.e)
NEG = -1e30
MESH = pl.DeviceIdType.MESH


def attend_rows(query, key_rows, value_rows, bias):
    scores = lax.dot_general(
        query, key_rows, (((1,), (1,)), ((), ())), preferred_element_type=jnp.float32
    )
    lows, totals = [], []
    for a in range(STEP // TILE):
        row = [
            scores[a * TILE : (a + 1) * TILE, b * TILE : (b + 1) * TILE] + bias(a, b)
            for b in range(ROWS // TILE)
        ]
        top = jnp.max(functools.reduce(jnp.maximum, row), axis=1, keepdims=True)
        weights = [jnp.exp2((part - top) * EXP_SCALE) for part in row]
        totals.append(jnp.sum(functools.reduce(jnp.add, weights), axis=1, keepdims=True))
        lows.append(jnp.concatenate([w.astype(jnp.bfloat16) for w in weights], axis=1))
    low = jnp.concatenate(lows, axis=0)
    total = jnp.concatenate(totals, axis=0)
    mixed = jnp.dot(low, value_rows, preferred_element_type=jnp.float32)
    return (mixed / total).astype(jnp.bfloat16)


def main_kernel(
    head_class, mask_s, mask_t, q_hbm, k_hbm, v_hbm, out,
    q_all, k_all, v_all, pack, recv, o_send, s_out, t_bias,
    in_sem, send_sem, recv_sem, o_send_sem, o_recv_sem, s_sem,
):
    me = lax.axis_index("seq")
    head = lax.axis_index("head")
    z, y, c = me // (NY * NC), (me // NC) % NY, me % NC

    def peer(i):
        dz, dy, dc = (i * 3) % NZ, (i // NZ) % NY, i // (NZ * NY)
        return ((z + dz) % NZ) * (NY * NC) + ((y + dy) % NY) * NC + (c + dc) % NC

    for n, (src, dst) in enumerate(((q_hbm, q_all), (k_hbm, k_all), (v_hbm, v_all))):
        for j in range(LOCAL_HEADS):
            cols = pl.ds(j * HEAD_DIM, HEAD_DIM)
            pltpu.make_async_copy(src.at[:, cols], dst.at[j], in_sem.at[n]).start()

    barrier = pltpu.get_barrier_semaphore()

    def greet(i, carry):
        pl.semaphore_signal(barrier, inc=1, device_id=(peer(i), head), device_id_type=MESH)
        return carry

    lax.fori_loop(1, SEQ, greet, 0)

    ranks, count_t, count_s = [], jnp.int32(0), jnp.int32(HT_DEV)
    for j in range(LOCAL_HEADS):
        is_t = head_class[j] > 0
        ranks.append(jnp.where(is_t, count_t, count_s))
        count_t = count_t + jnp.where(is_t, 1, 0)
        count_s = count_s + jnp.where(is_t, 0, 1)

    def head_of(n):
        place = jnp.int32(0)
        for j, rank in enumerate(ranks):
            place = jnp.where(rank == n, j, place)
        return place

    for n, whole in enumerate((q_all, k_all, v_all)):
        pltpu.make_async_copy(whole, whole, in_sem.at[n]).wait()

    def pack_head(t):
        place = head_of(t)
        for n, whole in enumerate((q_all, k_all, v_all)):
            pack[t, :, n] = whole[place].reshape(SEQ, PIECE, HEAD_DIM)

    def send_head(t):
        pltpu.make_async_copy(pack.at[t, me], recv.at[t, me], recv_sem.at[t]).start()

        def send(i, carry):
            other = peer(i)
            pltpu.make_async_remote_copy(
                src_ref=pack.at[t, other],
                dst_ref=recv.at[t, me],
                send_sem=send_sem.at[t],
                recv_sem=recv_sem.at[t],
                device_id=(other, head),
                device_id_type=MESH,
            ).start()
            return carry

        lax.fori_loop(1, SEQ, send, 0)

    pack_head(0)
    pl.semaphore_wait(barrier, SEQ - 1)
    send_head(0)
    for t in range(1, HT_DEV):
        pack_head(t)
        send_head(t)

    row = lax.broadcasted_iota(jnp.int32, (TILE, TILE), 0) % PIECE // 2
    col = lax.broadcasted_iota(jnp.int32, (TILE, TILE), 1) % PIECE // 2
    bias = jnp.full((TILE, TILE), NEG, jnp.float32)
    for g in range(mask_t.shape[0]):
        for i in range(2):
            for j in range(2):
                value = jnp.where(mask_t[g, i, j] > 0, 0.0, NEG).astype(jnp.float32)
                bias = jnp.where((row == 2 * g + i) & (col == 2 * g + j), value, bias)
    t_bias[...] = bias

    def spatial_head(n, carry):
        place = head_of(HT_DEV + n)

        def block(r, inner):
            at = pl.multiple_of(r * STEP, STEP)

            def tile_bias(a, b):
                allowed = mask_s[0, r * (STEP // TILE) + a, b] > 0
                return jnp.where(allowed, 0.0, NEG).astype(jnp.float32)

            s_out[n, pl.ds(at, STEP)] = attend_rows(
                q_all[place, pl.ds(at, STEP)], k_all[place], v_all[place], tile_bias
            )
            return inner

        lax.fori_loop(0, ROWS // STEP, block, 0)
        pltpu.make_async_copy(s_out.at[n], out.at[HT_DEV + n], s_sem.at[n]).start()
        return carry

    lax.fori_loop(0, HS_DEV, spatial_head, 0)

    def temporal_head(t, carry):
        pltpu.make_async_copy(recv.at[t], recv.at[t], recv_sem.at[t]).wait()

        def block(r, inner):
            frames = STEP // PIECE
            at = pl.ds(r * frames, frames)
            mixed = attend_rows(
                recv[t, at, 0].reshape(STEP, HEAD_DIM),
                recv[t, :, 1].reshape(ROWS, HEAD_DIM),
                recv[t, :, 2].reshape(ROWS, HEAD_DIM),
                lambda a, b: t_bias[...],
            )
            o_send[t, at] = mixed.reshape(frames, PIECE, HEAD_DIM)
            return inner

        lax.fori_loop(0, ROWS // STEP, block, 0)
        mine = pl.ds(pl.multiple_of(me * PIECE, PIECE), PIECE)
        pltpu.make_async_copy(o_send.at[t, me], out.at[t, mine], o_recv_sem.at[t]).start()

        def send(i, inner):
            other = peer(i)
            pltpu.make_async_remote_copy(
                src_ref=o_send.at[t, other],
                dst_ref=out.at[t, mine],
                send_sem=o_send_sem.at[t],
                recv_sem=o_recv_sem.at[t],
                device_id=(other, head),
                device_id_type=MESH,
            ).start()
            return inner

        lax.fori_loop(1, SEQ, send, 0)
        return carry

    lax.fori_loop(0, HT_DEV, temporal_head, 0)

    def finish(t, carry):
        sent = pack.at[t, pl.ds(0, SEQ - 1)]
        pltpu.make_async_copy(sent, sent, send_sem.at[t]).wait()
        sent = o_send.at[t, pl.ds(0, SEQ - 1)]
        pltpu.make_async_copy(sent, sent, o_send_sem.at[t]).wait()
        pltpu.make_async_copy(out.at[t], out.at[t], o_recv_sem.at[t]).wait()
        return carry

    def finish_spatial(n, carry):
        pltpu.make_async_copy(s_out.at[n], out.at[HT_DEV + n], s_sem.at[n]).wait()
        return carry

    lax.fori_loop(0, HS_DEV, finish_spatial, 0)
    lax.fori_loop(0, HT_DEV, finish, 0)


def place_kernel(head_class, packed, out, sem):
    count_t, count_s = jnp.int32(0), jnp.int32(HT_DEV)
    copies = []
    for j in range(LOCAL_HEADS):
        is_t = head_class[j] > 0
        rank = jnp.where(is_t, count_t, count_s)
        count_t = count_t + jnp.where(is_t, 1, 0)
        count_s = count_s + jnp.where(is_t, 0, 1)
        copy = pltpu.make_async_copy(
            packed.at[rank], out.at[:, pl.ds(j * HEAD_DIM, HEAD_DIM)], sem.at[j]
        )
        copy.start()
        copies.append(copy)
    for copy in copies:
        copy.wait()


def on_device(queries, keys, values, head_class, mask_spatial, mask_temporal):
    smem = pl.BlockSpec(memory_space=pltpu.SMEM)
    anywhere = pl.BlockSpec(memory_space=pl.ANY)
    whole = pltpu.VMEM((LOCAL_HEADS, ROWS, HEAD_DIM), jnp.bfloat16)
    moved = pltpu.VMEM((HT_DEV, SEQ, 3, PIECE, HEAD_DIM), jnp.bfloat16)
    packed = pl.pallas_call(
        main_kernel,
        out_shape=jax.ShapeDtypeStruct((LOCAL_HEADS, ROWS, HEAD_DIM), jnp.bfloat16),
        in_specs=[smem] * 3 + [anywhere] * 3,
        out_specs=anywhere,
        scratch_shapes=[
            whole, whole, whole, moved, moved,
            pltpu.VMEM((HT_DEV, SEQ, PIECE, HEAD_DIM), jnp.bfloat16),
            pltpu.VMEM((HS_DEV, ROWS, HEAD_DIM), jnp.bfloat16),
            pltpu.VMEM((TILE, TILE), jnp.float32),
            pltpu.SemaphoreType.DMA((3,)),
            pltpu.SemaphoreType.DMA((HT_DEV,)),
            pltpu.SemaphoreType.DMA((HT_DEV,)),
            pltpu.SemaphoreType.DMA((HT_DEV,)),
            pltpu.SemaphoreType.DMA((HT_DEV,)),
            pltpu.SemaphoreType.DMA((HS_DEV,)),
        ],
        compiler_params=pltpu.CompilerParams(
            collective_id=0, has_side_effects=True, vmem_limit_bytes=56 << 20
        ),
        cost_estimate=pl.CostEstimate(
            flops=10 * 4 * ROWS * ROWS * HEAD_DIM,
            bytes_accessed=10 << 20,
            transcendentals=10 * ROWS * ROWS,
        ),
        name="attend_and_move",
    )(head_class, mask_spatial, mask_temporal, queries, keys, values)
    return pl.pallas_call(
        place_kernel,
        out_shape=jax.ShapeDtypeStruct((ROWS, LOCAL_HEADS * HEAD_DIM), jnp.bfloat16),
        in_specs=[smem, anywhere],
        out_specs=anywhere,
        scratch_shapes=[pltpu.SemaphoreType.DMA((LOCAL_HEADS,))],
        name="place_heads",
    )(head_class, packed)


def solution(mesh):
    return jax.shard_map(
        on_device,
        mesh=mesh,
        in_specs=(
            P("seq", "head"),
            P("seq", "head"),
            P("seq", "head"),
            P("head"),
            P("seq", None, None),
            P("seq", None, None),
        ),
        out_specs=P("seq", "head"),
        check_vma=False,
    )
```

```python
import functools
import math

import jax
import jax.numpy as jnp
from jax import lax
from jax.experimental import pallas as pl
from jax.experimental.pallas import tpu as pltpu
from jax.sharding import PartitionSpec as P

HEAD_DIM = 128
TILE = 128
LOCAL_HEADS = 10
HT_DEV = 4
HS_DEV = LOCAL_HEADS - HT_DEV
ROWS = 1024
SEQ = 64
PIECE = ROWS // SEQ
NZ, NY, NC = 8, 4, 2
STEP = 256
EXP_SCALE = HEAD_DIM**-0.5 * math.log2(math.e)
NEG = -1e30
MESH = pl.DeviceIdType.MESH


def attend_rows(query, key_rows, value_rows, bias):
    scores = lax.dot_general(
        query, key_rows, (((1,), (1,)), ((), ())), preferred_element_type=jnp.float32
    )
    lows, totals = [], []
    for a in range(STEP // TILE):
        row = [
            scores[a * TILE : (a + 1) * TILE, b * TILE : (b + 1) * TILE] + bias(a, b)
            for b in range(ROWS // TILE)
        ]
        top = jnp.max(functools.reduce(jnp.maximum, row), axis=1, keepdims=True)
        weights = [jnp.exp2((part - top) * EXP_SCALE) for part in row]
        totals.append(jnp.sum(functools.reduce(jnp.add, weights), axis=1, keepdims=True))
        lows.append(jnp.concatenate([w.astype(jnp.bfloat16) for w in weights], axis=1))
    low = jnp.concatenate(lows, axis=0)
    total = jnp.concatenate(totals, axis=0)
    mixed = jnp.dot(low, value_rows, preferred_element_type=jnp.float32)
    return (mixed / total).astype(jnp.bfloat16)


def main_kernel(
    head_class, mask_s, mask_t, q_hbm, k_hbm, v_hbm, out,
    q_all, k_all, v_all, pack, recv, o_send, t_bias,
    in_sem, send_sem, recv_sem, o_send_sem, o_recv_sem,
):
    me = lax.axis_index("seq")
    head = lax.axis_index("head")
    z, y, c = me // (NY * NC), (me // NC) % NY, me % NC

    def peer(i):
        dz, dy, dc = (i * 3) % NZ, (i // NZ) % NY, i // (NZ * NY)
        return ((z + dz) % NZ) * (NY * NC) + ((y + dy) % NY) * NC + (c + dc) % NC

    for n, (src, dst) in enumerate(((q_hbm, q_all), (k_hbm, k_all), (v_hbm, v_all))):
        for j in range(LOCAL_HEADS):
            cols = pl.ds(j * HEAD_DIM, HEAD_DIM)
            pltpu.make_async_copy(src.at[:, cols], dst.at[j], in_sem.at[n]).start()

    barrier = pltpu.get_barrier_semaphore()

    def greet(i, carry):
        pl.semaphore_signal(barrier, inc=1, device_id=(peer(i), head), device_id_type=MESH)
        return carry

    lax.fori_loop(1, SEQ, greet, 0)

    ranks, count_t, count_s = [], jnp.int32(0), jnp.int32(HT_DEV)
    for j in range(LOCAL_HEADS):
        is_t = head_class[j] > 0
        ranks.append(jnp.where(is_t, count_t, count_s))
        count_t = count_t + jnp.where(is_t, 1, 0)
        count_s = count_s + jnp.where(is_t, 0, 1)

    def head_of(n):
        place = jnp.int32(0)
        for j, rank in enumerate(ranks):
            place = jnp.where(rank == n, j, place)
        return place

    for n, whole in enumerate((q_all, k_all, v_all)):
        pltpu.make_async_copy(whole, whole, in_sem.at[n]).wait()

    def pack_head(t):
        place = head_of(t)
        for n, whole in enumerate((q_all, k_all, v_all)):
            pack[t, :, n] = whole[place].reshape(SEQ, PIECE, HEAD_DIM)

    def send_head(t):
        pltpu.make_async_copy(pack.at[t, me], recv.at[t, me], recv_sem.at[t]).start()

        def send(i, carry):
            other = peer(i)
            pltpu.make_async_remote_copy(
                src_ref=pack.at[t, other],
                dst_ref=recv.at[t, me],
                send_sem=send_sem.at[t],
                recv_sem=recv_sem.at[t],
                device_id=(other, head),
                device_id_type=MESH,
            ).start()
            return carry

        lax.fori_loop(1, SEQ, send, 0)

    pack_head(0)
    pl.semaphore_wait(barrier, SEQ - 1)
    send_head(0)
    for t in range(1, HT_DEV):
        pack_head(t)
        send_head(t)

    row = lax.broadcasted_iota(jnp.int32, (TILE, TILE), 0) % PIECE // 2
    col = lax.broadcasted_iota(jnp.int32, (TILE, TILE), 1) % PIECE // 2
    bias = jnp.full((TILE, TILE), NEG, jnp.float32)
    for g in range(mask_t.shape[2]):
        for i in range(2):
            for j in range(2):
                value = jnp.where(mask_t[i, j, g] > 0, 0.0, NEG).astype(jnp.float32)
                bias = jnp.where((row == 2 * g + i) & (col == 2 * g + j), value, bias)
    t_bias[...] = bias

    def spatial_head(n, carry):
        place = head_of(HT_DEV + n)

        def block(r, inner):
            at = pl.multiple_of(r * STEP, STEP)

            def tile_bias(a, b):
                allowed = mask_s[0, r * (STEP // TILE) + a, b] > 0
                return jnp.where(allowed, 0.0, NEG).astype(jnp.float32)

            out[HT_DEV + n, pl.ds(at, STEP)] = attend_rows(
                q_all[place, pl.ds(at, STEP)], k_all[place], v_all[place], tile_bias
            )
            return inner

        lax.fori_loop(0, ROWS // STEP, block, 0)
        return carry

    lax.fori_loop(0, HS_DEV, spatial_head, 0)

    def temporal_head(t, carry):
        pltpu.make_async_copy(recv.at[t], recv.at[t], recv_sem.at[t]).wait()

        def block(r, inner):
            frames = STEP // PIECE
            at = pl.ds(r * frames, frames)
            mixed = attend_rows(
                recv[t, at, 0].reshape(STEP, HEAD_DIM),
                recv[t, :, 1].reshape(ROWS, HEAD_DIM),
                recv[t, :, 2].reshape(ROWS, HEAD_DIM),
                lambda a, b: t_bias[...],
            )
            o_send[t, at] = mixed.reshape(frames, PIECE, HEAD_DIM)
            return inner

        lax.fori_loop(0, ROWS // STEP, block, 0)
        mine = pl.ds(pl.multiple_of(me * PIECE, PIECE), PIECE)
        pltpu.make_async_copy(o_send.at[t, me], out.at[t, mine], o_recv_sem.at[t]).start()

        def send(i, inner):
            other = peer(i)
            pltpu.make_async_remote_copy(
                src_ref=o_send.at[t, other],
                dst_ref=out.at[t, mine],
                send_sem=o_send_sem.at[t],
                recv_sem=o_recv_sem.at[t],
                device_id=(other, head),
                device_id_type=MESH,
            ).start()
            return inner

        lax.fori_loop(1, SEQ, send, 0)
        return carry

    lax.fori_loop(0, HT_DEV, temporal_head, 0)

    def finish(t, carry):
        sent = pack.at[t, pl.ds(0, SEQ - 1)]
        pltpu.make_async_copy(sent, sent, send_sem.at[t]).wait()
        sent = o_send.at[t, pl.ds(0, SEQ - 1)]
        pltpu.make_async_copy(sent, sent, o_send_sem.at[t]).wait()
        pltpu.make_async_copy(out.at[t], out.at[t], o_recv_sem.at[t]).wait()
        return carry

    lax.fori_loop(0, HT_DEV, finish, 0)


def place_kernel(head_class, packed, out, sem):
    count_t, count_s = jnp.int32(0), jnp.int32(HT_DEV)
    copies = []
    for j in range(LOCAL_HEADS):
        is_t = head_class[j] > 0
        rank = jnp.where(is_t, count_t, count_s)
        count_t = count_t + jnp.where(is_t, 1, 0)
        count_s = count_s + jnp.where(is_t, 0, 1)
        copy = pltpu.make_async_copy(
            packed.at[rank], out.at[:, pl.ds(j * HEAD_DIM, HEAD_DIM)], sem.at[j]
        )
        copy.start()
        copies.append(copy)
    for copy in copies:
        copy.wait()


def on_device(queries, keys, values, head_class, mask_spatial, mask_temporal):
    smem = pl.BlockSpec(memory_space=pltpu.SMEM)
    anywhere = pl.BlockSpec(memory_space=pl.ANY)
    whole = pltpu.VMEM((LOCAL_HEADS, ROWS, HEAD_DIM), jnp.bfloat16)
    moved = pltpu.VMEM((HT_DEV, SEQ, 3, PIECE, HEAD_DIM), jnp.bfloat16)
    packed = pl.pallas_call(
        main_kernel,
        out_shape=pltpu.VMEM((LOCAL_HEADS, ROWS, HEAD_DIM), jnp.bfloat16),
        in_specs=[smem] * 3 + [anywhere] * 3,
        out_specs=pl.BlockSpec(memory_space=pltpu.VMEM),
        scratch_shapes=[
            whole, whole, whole, moved, moved,
            pltpu.VMEM((HT_DEV, SEQ, PIECE, HEAD_DIM), jnp.bfloat16),
            pltpu.VMEM((TILE, TILE), jnp.float32),
            pltpu.SemaphoreType.DMA((3,)),
            pltpu.SemaphoreType.DMA((HT_DEV,)),
            pltpu.SemaphoreType.DMA((HT_DEV,)),
            pltpu.SemaphoreType.DMA((HT_DEV,)),
            pltpu.SemaphoreType.DMA((HT_DEV,)),
        ],
        compiler_params=pltpu.CompilerParams(
            collective_id=0, has_side_effects=True, vmem_limit_bytes=60 << 20
        ),
        cost_estimate=pl.CostEstimate(
            flops=10 * 4 * ROWS * ROWS * HEAD_DIM,
            bytes_accessed=10 << 20,
            transcendentals=10 * ROWS * ROWS,
        ),
        name="attend_and_move",
    )(head_class, mask_spatial, jnp.transpose(mask_temporal, (1, 2, 0)), queries, keys, values)
    return pl.pallas_call(
        place_kernel,
        out_shape=jax.ShapeDtypeStruct((ROWS, LOCAL_HEADS * HEAD_DIM), jnp.bfloat16),
        in_specs=[smem, anywhere],
        out_specs=anywhere,
        scratch_shapes=[pltpu.SemaphoreType.DMA((LOCAL_HEADS,))],
        name="place_heads",
    )(head_class, packed)


def solution(mesh):
    return jax.shard_map(
        on_device,
        mesh=mesh,
        in_specs=(
            P("seq", "head"),
            P("seq", "head"),
            P("seq", "head"),
            P("head"),
            P("seq", None, None),
            P("seq", None, None),
        ),
        out_specs=P("seq", "head"),
        check_vma=False,
    )
```

```python
import functools
import math

import jax
import jax.numpy as jnp
from jax import lax
from jax.experimental import pallas as pl
from jax.experimental.pallas import tpu as pltpu
from jax.sharding import PartitionSpec as P

HEAD_DIM = 128
TILE = 128
LOCAL_HEADS = 10
HT_DEV = 4
HS_DEV = LOCAL_HEADS - HT_DEV
ROWS = 1024
SEQ = 64
PIECE = ROWS // SEQ
NZ, NY, NC = 8, 4, 2
STEP = 256
EXP_SCALE = HEAD_DIM**-0.5 * math.log2(math.e)
NEG = -1e30
MESH = pl.DeviceIdType.MESH


def attend_rows(query, key_rows, value_rows, bias):
    scores = lax.dot_general(
        query, key_rows, (((1,), (1,)), ((), ())), preferred_element_type=jnp.float32
    )
    lows, totals = [], []
    for a in range(STEP // TILE):
        row = [
            scores[a * TILE : (a + 1) * TILE, b * TILE : (b + 1) * TILE] + bias(a, b)
            for b in range(ROWS // TILE)
        ]
        top = jnp.max(functools.reduce(jnp.maximum, row), axis=1, keepdims=True)
        weights = [jnp.exp2((part - top) * EXP_SCALE) for part in row]
        totals.append(jnp.sum(functools.reduce(jnp.add, weights), axis=1, keepdims=True))
        lows.append(jnp.concatenate([w.astype(jnp.bfloat16) for w in weights], axis=1))
    low = jnp.concatenate(lows, axis=0)
    total = jnp.concatenate(totals, axis=0)
    mixed = jnp.dot(low, value_rows, preferred_element_type=jnp.float32)
    return (mixed / total).astype(jnp.bfloat16)


def main_kernel(
    head_class, mask_s, mask_t, q_hbm, k_hbm, v_hbm, out,
    q_all, k_all, v_all, pack, recv, o_send, t_bias,
    in_sem, send_sem, recv_sem, o_send_sem, o_recv_sem,
):
    me = lax.axis_index("seq")
    head = lax.axis_index("head")
    z, y, c = me // (NY * NC), (me // NC) % NY, me % NC

    def peer(i):
        dz, dy, dc = (i * 3) % NZ, (i // NZ) % NY, i // (NZ * NY)
        return ((z + dz) % NZ) * (NY * NC) + ((y + dy) % NY) * NC + (c + dc) % NC

    for n, (src, dst) in enumerate(((q_hbm, q_all), (k_hbm, k_all), (v_hbm, v_all))):
        for j in range(LOCAL_HEADS):
            cols = pl.ds(j * HEAD_DIM, HEAD_DIM)
            pltpu.make_async_copy(src.at[:, cols], dst.at[j], in_sem.at[n]).start()

    barrier = pltpu.get_barrier_semaphore()

    def greet(i, carry):
        pl.semaphore_signal(barrier, inc=1, device_id=(peer(i), head), device_id_type=MESH)
        return carry

    lax.fori_loop(1, SEQ, greet, 0)

    ranks, count_t, count_s = [], jnp.int32(0), jnp.int32(HT_DEV)
    for j in range(LOCAL_HEADS):
        is_t = head_class[j] > 0
        ranks.append(jnp.where(is_t, count_t, count_s))
        count_t = count_t + jnp.where(is_t, 1, 0)
        count_s = count_s + jnp.where(is_t, 0, 1)

    def head_of(n):
        place = jnp.int32(0)
        for j, rank in enumerate(ranks):
            place = jnp.where(rank == n, j, place)
        return place

    for n, whole in enumerate((q_all, k_all, v_all)):
        pltpu.make_async_copy(whole, whole, in_sem.at[n]).wait()

    def pack_head(t):
        place = head_of(t)
        for n, whole in enumerate((q_all, k_all, v_all)):
            pack[t, :, n] = whole[place].reshape(SEQ, PIECE, HEAD_DIM)

    def send_head(t):
        pltpu.make_async_copy(pack.at[t, me], recv.at[t, me], recv_sem.at[t]).start()

        def send(i, carry):
            other = peer(i)
            pltpu.make_async_remote_copy(
                src_ref=pack.at[t, other],
                dst_ref=recv.at[t, me],
                send_sem=send_sem.at[t],
                recv_sem=recv_sem.at[t],
                device_id=(other, head),
                device_id_type=MESH,
            ).start()
            return carry

        lax.fori_loop(1, SEQ, send, 0)

    pack_head(0)
    pl.semaphore_wait(barrier, SEQ - 1)
    send_head(0)
    for t in range(1, HT_DEV):
        pack_head(t)
        send_head(t)

    row = lax.broadcasted_iota(jnp.int32, (TILE, TILE), 0) % PIECE // 2
    col = lax.broadcasted_iota(jnp.int32, (TILE, TILE), 1) % PIECE // 2
    bias = jnp.full((TILE, TILE), NEG, jnp.float32)
    for g in range(mask_t.shape[2]):
        for i in range(2):
            for j in range(2):
                value = jnp.where(mask_t[i, j, g] > 0, 0.0, NEG).astype(jnp.float32)
                bias = jnp.where((row == 2 * g + i) & (col == 2 * g + j), value, bias)
    t_bias[...] = bias

    def spatial_head(n, carry):
        place = head_of(HT_DEV + n)

        def block(r, inner):
            at = pl.multiple_of(r * STEP, STEP)

            def tile_bias(a, b):
                allowed = mask_s[0, r * (STEP // TILE) + a, b] > 0
                return jnp.where(allowed, 0.0, NEG).astype(jnp.float32)

            out[HT_DEV + n, pl.ds(at, STEP)] = attend_rows(
                q_all[place, pl.ds(at, STEP)], k_all[place], v_all[place], tile_bias
            )
            return inner

        lax.fori_loop(0, ROWS // STEP, block, 0)
        return carry

    lax.fori_loop(0, HS_DEV, spatial_head, 0)

    def temporal_head(t, carry):
        pltpu.make_async_copy(recv.at[t], recv.at[t], recv_sem.at[t]).wait()

        def block(r, inner):
            frames = STEP // PIECE
            at = pl.ds(r * frames, frames)
            mixed = attend_rows(
                recv[t, at, 0].reshape(STEP, HEAD_DIM),
                recv[t, :, 1].reshape(ROWS, HEAD_DIM),
                recv[t, :, 2].reshape(ROWS, HEAD_DIM),
                lambda a, b: t_bias[...],
            )
            o_send[t, at] = mixed.reshape(frames, PIECE, HEAD_DIM)
            return inner

        lax.fori_loop(0, ROWS // STEP, block, 0)
        mine = pl.ds(pl.multiple_of(me * PIECE, PIECE), PIECE)
        pltpu.make_async_copy(o_send.at[t, me], out.at[t, mine], o_recv_sem.at[t]).start()

        def send(i, inner):
            other = peer(i)
            pltpu.make_async_remote_copy(
                src_ref=o_send.at[t, other],
                dst_ref=out.at[t, mine],
                send_sem=o_send_sem.at[t],
                recv_sem=o_recv_sem.at[t],
                device_id=(other, head),
                device_id_type=MESH,
            ).start()
            return inner

        lax.fori_loop(1, SEQ, send, 0)
        return carry

    lax.fori_loop(0, HT_DEV, temporal_head, 0)

    def finish(t, carry):
        sent = pack.at[t, pl.ds(0, SEQ - 1)]
        pltpu.make_async_copy(sent, sent, send_sem.at[t]).wait()
        sent = o_send.at[t, pl.ds(0, SEQ - 1)]
        pltpu.make_async_copy(sent, sent, o_send_sem.at[t]).wait()
        pltpu.make_async_copy(out.at[t], out.at[t], o_recv_sem.at[t]).wait()
        return carry

    lax.fori_loop(0, HT_DEV, finish, 0)


def place_kernel(head_class, packed, out, sem):
    count_t, count_s = jnp.int32(0), jnp.int32(HT_DEV)
    copies = []
    for j in range(LOCAL_HEADS):
        is_t = head_class[j] > 0
        rank = jnp.where(is_t, count_t, count_s)
        count_t = count_t + jnp.where(is_t, 1, 0)
        count_s = count_s + jnp.where(is_t, 0, 1)
        copy = pltpu.make_async_copy(
            packed.at[rank], out.at[:, pl.ds(j * HEAD_DIM, HEAD_DIM)], sem.at[j]
        )
        copy.start()
        copies.append(copy)
    for copy in copies:
        copy.wait()


def on_device(queries, keys, values, head_class, mask_spatial, mask_temporal):
    smem = pl.BlockSpec(memory_space=pltpu.SMEM)
    anywhere = pl.BlockSpec(memory_space=pl.ANY)
    whole = pltpu.VMEM((LOCAL_HEADS, ROWS, HEAD_DIM), jnp.bfloat16)
    moved = pltpu.VMEM((HT_DEV, SEQ, 3, PIECE, HEAD_DIM), jnp.bfloat16)
    packed = pl.pallas_call(
        main_kernel,
        out_shape=pltpu.VMEM((LOCAL_HEADS, ROWS, HEAD_DIM), jnp.bfloat16),
        in_specs=[smem] * 3 + [anywhere] * 3,
        out_specs=pl.BlockSpec(memory_space=pltpu.VMEM),
        scratch_shapes=[
            whole, whole, whole, moved, moved,
            pltpu.VMEM((HT_DEV, SEQ, PIECE, HEAD_DIM), jnp.bfloat16),
            pltpu.VMEM((TILE, TILE), jnp.float32),
            pltpu.SemaphoreType.DMA((3,)),
            pltpu.SemaphoreType.DMA((HT_DEV,)),
            pltpu.SemaphoreType.DMA((HT_DEV,)),
            pltpu.SemaphoreType.DMA((HT_DEV,)),
            pltpu.SemaphoreType.DMA((HT_DEV,)),
        ],
        compiler_params=pltpu.CompilerParams(
            collective_id=0, has_side_effects=True, vmem_limit_bytes=60 << 20
        ),
        cost_estimate=pl.CostEstimate(
            flops=10 * 4 * ROWS * ROWS * HEAD_DIM,
            bytes_accessed=10 << 20,
            transcendentals=10 * ROWS * ROWS,
        ),
        name="attend_and_move",
    )(head_class, mask_spatial, jnp.transpose(mask_temporal, (1, 2, 0)), queries, keys, values)
    return pl.pallas_call(
        place_kernel,
        out_shape=jax.ShapeDtypeStruct((ROWS, LOCAL_HEADS * HEAD_DIM), jnp.bfloat16),
        in_specs=[smem, anywhere],
        out_specs=anywhere,
        scratch_shapes=[pltpu.SemaphoreType.DMA((LOCAL_HEADS,))],
        compiler_params=pltpu.CompilerParams(vmem_limit_bytes=8 << 20),
        name="place_heads",
    )(head_class, pltpu.with_memory_space_constraint(packed, pltpu.VMEM))


def solution(mesh):
    return jax.shard_map(
        on_device,
        mesh=mesh,
        in_specs=(
            P("seq", "head"),
            P("seq", "head"),
            P("seq", "head"),
            P("head"),
            P("seq", None, None),
            P("seq", None, None),
        ),
        out_specs=P("seq", "head"),
        check_vma=False,
    )
```

```python
import functools
import math

import jax
import jax.numpy as jnp
from jax import lax
from jax.experimental import pallas as pl
from jax.experimental.pallas import tpu as pltpu
from jax.sharding import PartitionSpec as P

HEAD_DIM = 128
TILE = 128
LOCAL_HEADS = 10
HT_DEV = 4
HS_DEV = LOCAL_HEADS - HT_DEV
ROWS = 1024
SEQ = 64
PIECE = ROWS // SEQ
NZ, NY, NC = 8, 4, 2
STEP = 256
EXP_SCALE = HEAD_DIM**-0.5 * math.log2(math.e)
NEG = -1e30
MESH = pl.DeviceIdType.MESH


def attend_rows(query, key_rows, value_rows, bias):
    scores = lax.dot_general(
        query, key_rows, (((1,), (1,)), ((), ())), preferred_element_type=jnp.float32
    )
    lows, totals = [], []
    for a in range(STEP // TILE):
        row = [
            scores[a * TILE : (a + 1) * TILE, b * TILE : (b + 1) * TILE] + bias(a, b)
            for b in range(ROWS // TILE)
        ]
        top = jnp.max(functools.reduce(jnp.maximum, row), axis=1, keepdims=True)
        weights = [jnp.exp2((part - top) * EXP_SCALE) for part in row]
        totals.append(jnp.sum(functools.reduce(jnp.add, weights), axis=1, keepdims=True))
        lows.append(jnp.concatenate([w.astype(jnp.bfloat16) for w in weights], axis=1))
    low = jnp.concatenate(lows, axis=0)
    total = jnp.concatenate(totals, axis=0)
    mixed = jnp.dot(low, value_rows, preferred_element_type=jnp.float32)
    return (mixed / total).astype(jnp.bfloat16)


def main_kernel(
    head_class, mask_s, mask_t, q_hbm, k_hbm, v_hbm, out,
    q_all, k_all, v_all, k_pack, v_pack, q_pack, k_got, v_got, q_got, o_send, t_bias,
    in_sem, kv_send_sem, kv_recv_sem, q_send_sem, q_recv_sem, o_send_sem, o_recv_sem,
):
    me = lax.axis_index("seq")
    head = lax.axis_index("head")
    z, y, c = lax.div(me, NY * NC), lax.rem(lax.div(me, NC), NY), lax.rem(me, NC)
    z_part = [lax.rem(z + step, NZ) * (NY * NC) for step in (4, 3, 5, 2, 6, 1, 7, 0)]

    def plane(i):
        return lax.rem(y + lax.div(i, NC), NY) * NC + lax.rem(c + lax.rem(i, NC), NC)

    def every_peer(act):
        for part in z_part[:-1]:
            act(part + y * NC + c)

        def others(i, carry):
            rest = plane(i)
            for part in z_part:
                act(part + rest)
            return carry

        lax.fori_loop(1, NY * NC, others, 0)

    def load(n, src, dst):
        for j in range(LOCAL_HEADS):
            cols = pl.ds(j * HEAD_DIM, HEAD_DIM)
            pltpu.make_async_copy(src.at[:, cols], dst.at[j], in_sem.at[n]).start()

    def loaded(n, dst):
        pltpu.make_async_copy(dst, dst, in_sem.at[n]).wait()

    def arrived(got, sem):
        pltpu.make_async_copy(got, got, sem).wait()

    def send_all(src, dst, mine, send_sem, recv_sem):
        pltpu.make_async_copy(src(me), mine, recv_sem).start()

        def send(other):
            pltpu.make_async_remote_copy(
                src_ref=src(other),
                dst_ref=dst,
                send_sem=send_sem,
                recv_sem=recv_sem,
                device_id=(other, head),
                device_id_type=MESH,
            ).start()

        every_peer(send)

    load(1, k_hbm, k_all)

    barrier = pltpu.get_barrier_semaphore()
    for i in range(NY * NC):
        rest = plane(i)
        for part in z_part if i else z_part[:-1]:
            pl.semaphore_signal(
                barrier, inc=1, device_id=(part + rest, head), device_id_type=MESH
            )

    load(2, v_hbm, v_all)
    load(0, q_hbm, q_all)

    ranks, count_t, count_s = [], jnp.int32(0), jnp.int32(HT_DEV)
    for j in range(LOCAL_HEADS):
        is_t = head_class[j] > 0
        ranks.append(jnp.where(is_t, count_t, count_s))
        count_t = count_t + jnp.where(is_t, 1, 0)
        count_s = count_s + jnp.where(is_t, 0, 1)

    def head_of(n):
        place = jnp.int32(0)
        for j, rank in enumerate(ranks):
            place = jnp.where(rank == n, j, place)
        return place

    places = [head_of(t) for t in range(HT_DEV)]

    loaded(1, k_all)
    for t, place in enumerate(places):
        k_pack[:, t] = k_all[place].reshape(SEQ, PIECE, HEAD_DIM)
    pl.semaphore_wait(barrier, SEQ - 1)
    send_all(
        lambda s: k_pack.at[s], k_got.at[me], k_got.at[me], kv_send_sem.at[0], kv_recv_sem.at[0]
    )
    loaded(2, v_all)
    for t, place in enumerate(places):
        v_pack[:, t] = v_all[place].reshape(SEQ, PIECE, HEAD_DIM)
    send_all(
        lambda s: v_pack.at[s], v_got.at[me], v_got.at[me], kv_send_sem.at[1], kv_recv_sem.at[1]
    )
    loaded(0, q_all)
    for t, place in enumerate(places):
        q_pack[t] = q_all[place].reshape(SEQ, PIECE, HEAD_DIM)

    def send_queries(t, carry):
        send_all(
            lambda s: q_pack.at[t, s], q_got.at[t, me], q_got.at[t, me],
            q_send_sem.at[t], q_recv_sem.at[t],
        )
        return carry

    lax.fori_loop(0, HT_DEV, send_queries, 0)

    row = lax.broadcasted_iota(jnp.int32, (TILE, TILE), 0) % PIECE // 2
    col = lax.broadcasted_iota(jnp.int32, (TILE, TILE), 1) % PIECE // 2
    bias = jnp.full((TILE, TILE), NEG, jnp.float32)
    for g in range(mask_t.shape[2]):
        for i in range(2):
            for j in range(2):
                value = jnp.where(mask_t[i, j, g] > 0, 0.0, NEG).astype(jnp.float32)
                bias = jnp.where((row == 2 * g + i) & (col == 2 * g + j), value, bias)
    t_bias[...] = bias

    def spatial_head(n, carry):
        place = head_of(HT_DEV + n)

        def block(r, inner):
            at = pl.multiple_of(r * STEP, STEP)

            def tile_bias(a, b):
                allowed = mask_s[0, r * (STEP // TILE) + a, b] > 0
                return jnp.where(allowed, 0.0, NEG).astype(jnp.float32)

            out[HT_DEV + n, pl.ds(at, STEP)] = attend_rows(
                q_all[place, pl.ds(at, STEP)], k_all[place], v_all[place], tile_bias
            )
            return inner

        lax.fori_loop(0, ROWS // STEP, block, 0)
        return carry

    lax.fori_loop(0, HS_DEV, spatial_head, 0)

    arrived(k_got, kv_recv_sem.at[0])
    arrived(v_got, kv_recv_sem.at[1])

    def temporal_head(t, carry):
        arrived(q_got.at[t], q_recv_sem.at[t])

        def block(r, inner):
            frames = STEP // PIECE
            at = pl.ds(r * frames, frames)
            mixed = attend_rows(
                q_got[t, at].reshape(STEP, HEAD_DIM),
                k_got[:, t].reshape(ROWS, HEAD_DIM),
                v_got[:, t].reshape(ROWS, HEAD_DIM),
                lambda a, b: t_bias[...],
            )
            o_send[t, at] = mixed.reshape(frames, PIECE, HEAD_DIM)
            return inner

        lax.fori_loop(0, ROWS // STEP, block, 0)
        mine = out.at[t, pl.ds(pl.multiple_of(me * PIECE, PIECE), PIECE)]
        send_all(lambda s: o_send.at[t, s], mine, mine, o_send_sem.at[t], o_recv_sem.at[t])
        return carry

    lax.fori_loop(0, HT_DEV, temporal_head, 0)

    others = pl.ds(0, SEQ - 1)
    arrived(k_pack.at[others], kv_send_sem.at[0])
    arrived(v_pack.at[others], kv_send_sem.at[1])

    def finish(t, carry):
        arrived(q_pack.at[t, others], q_send_sem.at[t])
        arrived(o_send.at[t, others], o_send_sem.at[t])
        arrived(out.at[t], o_recv_sem.at[t])
        return carry

    lax.fori_loop(0, HT_DEV, finish, 0)


def place_kernel(head_class, packed, out, sem):
    count_t, count_s = jnp.int32(0), jnp.int32(HT_DEV)
    copies = []
    for j in range(LOCAL_HEADS):
        is_t = head_class[j] > 0
        rank = jnp.where(is_t, count_t, count_s)
        count_t = count_t + jnp.where(is_t, 1, 0)
        count_s = count_s + jnp.where(is_t, 0, 1)
        copy = pltpu.make_async_copy(
            packed.at[rank], out.at[:, pl.ds(j * HEAD_DIM, HEAD_DIM)], sem.at[j]
        )
        copy.start()
        copies.append(copy)
    for copy in copies:
        copy.wait()


def on_device(queries, keys, values, head_class, mask_spatial, mask_temporal):
    smem = pl.BlockSpec(memory_space=pltpu.SMEM)
    anywhere = pl.BlockSpec(memory_space=pl.ANY)
    whole = pltpu.VMEM((LOCAL_HEADS, ROWS, HEAD_DIM), jnp.bfloat16)
    by_device = pltpu.VMEM((SEQ, HT_DEV, PIECE, HEAD_DIM), jnp.bfloat16)
    by_head = pltpu.VMEM((HT_DEV, SEQ, PIECE, HEAD_DIM), jnp.bfloat16)
    packed = pl.pallas_call(
        main_kernel,
        out_shape=pltpu.VMEM((LOCAL_HEADS, ROWS, HEAD_DIM), jnp.bfloat16),
        in_specs=[smem] * 3 + [anywhere] * 3,
        out_specs=pl.BlockSpec(memory_space=pltpu.VMEM),
        scratch_shapes=[
            whole, whole, whole,
            by_device, by_device, by_head, by_device, by_device, by_head, by_head,
            pltpu.VMEM((TILE, TILE), jnp.float32),
            pltpu.SemaphoreType.DMA((3,)),
            pltpu.SemaphoreType.DMA((2,)),
            pltpu.SemaphoreType.DMA((2,)),
            pltpu.SemaphoreType.DMA((HT_DEV,)),
            pltpu.SemaphoreType.DMA((HT_DEV,)),
            pltpu.SemaphoreType.DMA((HT_DEV,)),
            pltpu.SemaphoreType.DMA((HT_DEV,)),
        ],
        compiler_params=pltpu.CompilerParams(
            collective_id=0, has_side_effects=True, vmem_limit_bytes=60 << 20
        ),
        cost_estimate=pl.CostEstimate(
            flops=10 * 4 * ROWS * ROWS * HEAD_DIM,
            bytes_accessed=10 << 20,
            transcendentals=10 * ROWS * ROWS,
        ),
        name="attend_and_move",
    )(head_class, mask_spatial, jnp.transpose(mask_temporal, (1, 2, 0)), queries, keys, values)
    return pl.pallas_call(
        place_kernel,
        out_shape=jax.ShapeDtypeStruct((ROWS, LOCAL_HEADS * HEAD_DIM), jnp.bfloat16),
        in_specs=[smem, anywhere],
        out_specs=anywhere,
        scratch_shapes=[pltpu.SemaphoreType.DMA((LOCAL_HEADS,))],
        compiler_params=pltpu.CompilerParams(vmem_limit_bytes=8 << 20),
        name="place_heads",
    )(head_class, pltpu.with_memory_space_constraint(packed, pltpu.VMEM))


def solution(mesh):
    return jax.shard_map(
        on_device,
        mesh=mesh,
        in_specs=(
            P("seq", "head"),
            P("seq", "head"),
            P("seq", "head"),
            P("head"),
            P("seq", None, None),
            P("seq", None, None),
        ),
        out_specs=P("seq", "head"),
        check_vma=False,
    )
```

```python
import functools
import math

import jax
import jax.numpy as jnp
from jax import lax
from jax.experimental import pallas as pl
from jax.experimental.pallas import tpu as pltpu
from jax.sharding import PartitionSpec as P

HEAD_DIM = 128
TILE = 128
LOCAL_HEADS = 10
HT_DEV = 4
HS_DEV = LOCAL_HEADS - HT_DEV
ROWS = 1024
SEQ = 64
PIECE = ROWS // SEQ
NZ, NY, NC = 8, 4, 2
STEP = 256
EXP_SCALE = HEAD_DIM**-0.5 * math.log2(math.e)
NEG = -1e30
MESH = pl.DeviceIdType.MESH


def attend_rows(query, key_rows, value_rows, bias):
    scores = lax.dot_general(
        query, key_rows, (((1,), (1,)), ((), ())), preferred_element_type=jnp.float32
    )
    lows, totals = [], []
    for a in range(STEP // TILE):
        row = [
            scores[a * TILE : (a + 1) * TILE, b * TILE : (b + 1) * TILE] + bias(a, b)
            for b in range(ROWS // TILE)
        ]
        top = jnp.max(functools.reduce(jnp.maximum, row), axis=1, keepdims=True)
        weights = [jnp.exp2((part - top) * EXP_SCALE) for part in row]
        totals.append(jnp.sum(functools.reduce(jnp.add, weights), axis=1, keepdims=True))
        lows.append(jnp.concatenate([w.astype(jnp.bfloat16) for w in weights], axis=1))
    low = jnp.concatenate(lows, axis=0)
    total = jnp.concatenate(totals, axis=0)
    mixed = jnp.dot(low, value_rows, preferred_element_type=jnp.float32)
    return (mixed / total).astype(jnp.bfloat16)


def main_kernel(
    head_class_hbm, mask_s_hbm, mask_t_hbm, q_hbm, k_hbm, v_hbm, out,
    head_class, mask_s, mask_t, q_all, k_all, v_all, k_pack, v_pack, q_pack, k_got, v_got, q_got, o_send, t_bias,
    small_sem, in_sem, plane_sem, kv_send_sem, kv_recv_sem, q_send_sem, q_recv_sem, o_send_sem, o_recv_sem,
):
    me = lax.axis_index("seq")
    head = lax.axis_index("head")
    z, y, c = lax.div(me, NY * NC), lax.rem(lax.div(me, NC), NY), lax.rem(me, NC)
    z_part = [lax.rem(z + step, NZ) * (NY * NC) for step in (4, 3, 5, 2, 6, 1, 7, 0)]

    def plane(i):
        return lax.rem(y + lax.div(i, NC), NY) * NC + lax.rem(c + lax.rem(i, NC), NC)

    own_plane = [z_part[-1] + plane(i) for i in range(1, NY * NC)]
    near = [part + y * NC + c for part in z_part[:-1]] + own_plane

    def far_peers(act):
        def others(i, carry):
            rest = plane(i)
            for part in z_part[:-1]:
                act(part + rest)
            return carry

        lax.fori_loop(1, NY * NC, others, 0)

    def load(n, src, dst):
        for j in range(LOCAL_HEADS):
            cols = pl.ds(j * HEAD_DIM, HEAD_DIM)
            pltpu.make_async_copy(src.at[:, cols], dst.at[j], in_sem.at[n]).start()

    def loaded(n, dst):
        pltpu.make_async_copy(dst, dst, in_sem.at[n]).wait()

    def arrived(got, sem):
        pltpu.make_async_copy(got, got, sem).wait()

    def send_all(src, dst, mine, send_sem, recv_sem, between=lambda: None):
        pltpu.make_async_copy(src(me), mine, recv_sem).start()

        def send(other):
            pltpu.make_async_remote_copy(
                src_ref=src(other),
                dst_ref=dst,
                send_sem=send_sem,
                recv_sem=recv_sem,
                device_id=(other, head),
                device_id_type=MESH,
            ).start()

        for other in near:
            send(other)
        between()
        far_peers(send)

    smalls = [
        pltpu.make_async_copy(src, dst, small_sem.at[n])
        for n, (src, dst) in enumerate(
            ((head_class_hbm, head_class), (mask_s_hbm, mask_s), (mask_t_hbm, mask_t))
        )
    ]
    smalls[0].start()
    load(1, k_hbm, k_all)

    barrier = pltpu.get_barrier_semaphore()
    for other in near:
        pl.semaphore_signal(barrier, inc=1, device_id=(other, head), device_id_type=MESH)
    for small in smalls[1:]:
        small.start()
    smalls[0].wait()

    ranks, count_t, count_s = [], jnp.int32(0), jnp.int32(HT_DEV)
    for j in range(LOCAL_HEADS):
        is_t = head_class[j] > 0
        ranks.append(jnp.where(is_t, count_t, count_s))
        count_t = count_t + jnp.where(is_t, 1, 0)
        count_s = count_s + jnp.where(is_t, 0, 1)

    def head_of(n):
        place = jnp.int32(0)
        for j, rank in enumerate(ranks):
            place = jnp.where(rank == n, j, place)
        return place

    places = [head_of(t) for t in range(HT_DEV)]

    pl.semaphore_wait(barrier, len(near))
    for other in own_plane:
        pl.semaphore_signal(plane_sem, inc=1, device_id=(other, head), device_id_type=MESH)

    loaded(1, k_all)
    for t, place in enumerate(places):
        k_pack[:, t] = k_all[place].reshape(SEQ, PIECE, HEAD_DIM)
    send_all(
        lambda s: k_pack.at[s], k_got.at[me], k_got.at[me], kv_send_sem.at[0], kv_recv_sem.at[0],
        between=lambda: pl.semaphore_wait(plane_sem, len(own_plane)),
    )
    load(2, v_hbm, v_all)
    load(0, q_hbm, q_all)
    loaded(2, v_all)
    for t, place in enumerate(places):
        v_pack[:, t] = v_all[place].reshape(SEQ, PIECE, HEAD_DIM)
    send_all(
        lambda s: v_pack.at[s], v_got.at[me], v_got.at[me], kv_send_sem.at[1], kv_recv_sem.at[1]
    )
    loaded(0, q_all)
    for t, place in enumerate(places):
        q_pack[t] = q_all[place].reshape(SEQ, PIECE, HEAD_DIM)

    def send_queries(t, carry):
        send_all(
            lambda s: q_pack.at[t, s], q_got.at[t, me], q_got.at[t, me],
            q_send_sem.at[t], q_recv_sem.at[t],
        )
        return carry

    lax.fori_loop(0, HT_DEV, send_queries, 0)

    for small in smalls[1:]:
        small.wait()
    row = lax.broadcasted_iota(jnp.int32, (TILE, TILE), 0) % PIECE // 2
    col = lax.broadcasted_iota(jnp.int32, (TILE, TILE), 1) % PIECE // 2
    bias = jnp.full((TILE, TILE), NEG, jnp.float32)
    for g in range(mask_t.shape[2]):
        for i in range(2):
            for j in range(2):
                value = jnp.where(mask_t[i, j, g] > 0, 0.0, NEG).astype(jnp.float32)
                bias = jnp.where((row == 2 * g + i) & (col == 2 * g + j), value, bias)
    t_bias[...] = bias

    def spatial_head(n, carry):
        place = head_of(HT_DEV + n)

        def block(r, inner):
            at = pl.multiple_of(r * STEP, STEP)

            def tile_bias(a, b):
                allowed = mask_s[0, r * (STEP // TILE) + a, b] > 0
                return jnp.where(allowed, 0.0, NEG).astype(jnp.float32)

            out[HT_DEV + n, pl.ds(at, STEP)] = attend_rows(
                q_all[place, pl.ds(at, STEP)], k_all[place], v_all[place], tile_bias
            )
            return inner

        lax.fori_loop(0, ROWS // STEP, block, 0)
        return carry

    lax.fori_loop(0, HS_DEV, spatial_head, 0)

    arrived(k_got, kv_recv_sem.at[0])
    arrived(v_got, kv_recv_sem.at[1])

    def temporal_head(t, carry):
        arrived(q_got.at[t], q_recv_sem.at[t])

        def block(r, inner):
            frames = STEP // PIECE
            at = pl.ds(r * frames, frames)
            mixed = attend_rows(
                q_got[t, at].reshape(STEP, HEAD_DIM),
                k_got[:, t].reshape(ROWS, HEAD_DIM),
                v_got[:, t].reshape(ROWS, HEAD_DIM),
                lambda a, b: t_bias[...],
            )
            o_send[t, at] = mixed.reshape(frames, PIECE, HEAD_DIM)
            return inner

        lax.fori_loop(0, ROWS // STEP, block, 0)
        mine = out.at[t, pl.ds(pl.multiple_of(me * PIECE, PIECE), PIECE)]
        send_all(lambda s: o_send.at[t, s], mine, mine, o_send_sem.at[t], o_recv_sem.at[t])
        return carry

    lax.fori_loop(0, HT_DEV, temporal_head, 0)

    others = pl.ds(0, SEQ - 1)
    arrived(k_pack.at[others], kv_send_sem.at[0])
    arrived(v_pack.at[others], kv_send_sem.at[1])

    def finish(t, carry):
        arrived(q_pack.at[t, others], q_send_sem.at[t])
        arrived(o_send.at[t, others], o_send_sem.at[t])
        arrived(out.at[t], o_recv_sem.at[t])
        return carry

    lax.fori_loop(0, HT_DEV, finish, 0)


def place_kernel(head_class, packed, out, sem):
    count_t, count_s = jnp.int32(0), jnp.int32(HT_DEV)
    copies = []
    for j in range(LOCAL_HEADS):
        is_t = head_class[j] > 0
        rank = jnp.where(is_t, count_t, count_s)
        count_t = count_t + jnp.where(is_t, 1, 0)
        count_s = count_s + jnp.where(is_t, 0, 1)
        copy = pltpu.make_async_copy(
            packed.at[rank], out.at[:, pl.ds(j * HEAD_DIM, HEAD_DIM)], sem.at[j]
        )
        copy.start()
        copies.append(copy)
    for copy in copies:
        copy.wait()


def on_device(queries, keys, values, head_class, mask_spatial, mask_temporal):
    smem = pl.BlockSpec(memory_space=pltpu.SMEM)
    anywhere = pl.BlockSpec(memory_space=pl.ANY)
    whole = pltpu.VMEM((LOCAL_HEADS, ROWS, HEAD_DIM), jnp.bfloat16)
    by_device = pltpu.VMEM((SEQ, HT_DEV, PIECE, HEAD_DIM), jnp.bfloat16)
    by_head = pltpu.VMEM((HT_DEV, SEQ, PIECE, HEAD_DIM), jnp.bfloat16)
    packed = pl.pallas_call(
        main_kernel,
        out_shape=pltpu.VMEM((LOCAL_HEADS, ROWS, HEAD_DIM), jnp.bfloat16),
        in_specs=[anywhere] * 6,
        out_specs=pl.BlockSpec(memory_space=pltpu.VMEM),
        scratch_shapes=[
            pltpu.SMEM(head_class.shape, jnp.int32),
            pltpu.SMEM(mask_spatial.shape, jnp.int32),
            pltpu.SMEM(mask_temporal.shape[1:] + mask_temporal.shape[:1], jnp.int32),
            whole, whole, whole,
            by_device, by_device, by_head, by_device, by_device, by_head, by_head,
            pltpu.VMEM((TILE, TILE), jnp.float32),
            pltpu.SemaphoreType.DMA((3,)),
            pltpu.SemaphoreType.DMA((3,)),
            pltpu.SemaphoreType.REGULAR,
            pltpu.SemaphoreType.DMA((2,)),
            pltpu.SemaphoreType.DMA((2,)),
            pltpu.SemaphoreType.DMA((HT_DEV,)),
            pltpu.SemaphoreType.DMA((HT_DEV,)),
            pltpu.SemaphoreType.DMA((HT_DEV,)),
            pltpu.SemaphoreType.DMA((HT_DEV,)),
        ],
        compiler_params=pltpu.CompilerParams(
            collective_id=0, has_side_effects=True, vmem_limit_bytes=60 << 20
        ),
        cost_estimate=pl.CostEstimate(
            flops=10 * 4 * ROWS * ROWS * HEAD_DIM,
            bytes_accessed=10 << 20,
            transcendentals=10 * ROWS * ROWS,
        ),
        name="attend_and_move",
    )(head_class, mask_spatial, jnp.transpose(mask_temporal, (1, 2, 0)), queries, keys, values)
    return pl.pallas_call(
        place_kernel,
        out_shape=jax.ShapeDtypeStruct((ROWS, LOCAL_HEADS * HEAD_DIM), jnp.bfloat16),
        in_specs=[smem, anywhere],
        out_specs=anywhere,
        scratch_shapes=[pltpu.SemaphoreType.DMA((LOCAL_HEADS,))],
        compiler_params=pltpu.CompilerParams(vmem_limit_bytes=8 << 20),
        name="place_heads",
    )(head_class, pltpu.with_memory_space_constraint(packed, pltpu.VMEM))


def solution(mesh):
    return jax.shard_map(
        on_device,
        mesh=mesh,
        in_specs=(
            P("seq", "head"),
            P("seq", "head"),
            P("seq", "head"),
            P("head"),
            P("seq", None, None),
            P("seq", None, None),
        ),
        out_specs=P("seq", "head"),
        check_vma=False,
    )
```

```python
import functools
import math

import jax
import jax.numpy as jnp
from jax import lax
from jax.experimental import pallas as pl
from jax.experimental.pallas import tpu as pltpu
from jax.sharding import PartitionSpec as P

HEAD_DIM = 128
TILE = 128
LOCAL_HEADS = 10
HT_DEV = 4
HS_DEV = LOCAL_HEADS - HT_DEV
ROWS = 1024
SEQ = 64
PIECE = ROWS // SEQ
NZ, NY, NC = 8, 4, 2
STEP = 256
EXP_SCALE = HEAD_DIM**-0.5 * math.log2(math.e)
NEG = -1e30
MESH = pl.DeviceIdType.MESH


def attend_rows(query, key_rows, value_rows, bias):
    scores = lax.dot_general(
        query, key_rows, (((1,), (1,)), ((), ())), preferred_element_type=jnp.float32
    )
    lows, totals = [], []
    for a in range(STEP // TILE):
        row = [
            scores[a * TILE : (a + 1) * TILE, b * TILE : (b + 1) * TILE] + bias(a, b)
            for b in range(ROWS // TILE)
        ]
        top = jnp.max(functools.reduce(jnp.maximum, row), axis=1, keepdims=True)
        weights = [jnp.exp2((part - top) * EXP_SCALE) for part in row]
        totals.append(jnp.sum(functools.reduce(jnp.add, weights), axis=1, keepdims=True))
        lows.append(jnp.concatenate([w.astype(jnp.bfloat16) for w in weights], axis=1))
    low = jnp.concatenate(lows, axis=0)
    total = jnp.concatenate(totals, axis=0)
    mixed = jnp.dot(low, value_rows, preferred_element_type=jnp.float32)
    return (mixed / total).astype(jnp.bfloat16)


def main_kernel(
    head_class_hbm, mask_s_hbm, mask_t_hbm, q_hbm, k_hbm, v_hbm, out,
    head_class, mask_s, mask_t, q_all, k_all, v_all, k_pack, v_pack, q_pack, k_got, v_got, q_got, o_send, t_bias,
    small_sem, in_sem, plane_sem, kv_send_sem, kv_recv_sem, q_send_sem, q_recv_sem, o_send_sem, o_recv_sem,
):
    me = lax.axis_index("seq")
    head = lax.axis_index("head")
    z, y, c = lax.div(me, NY * NC), lax.rem(lax.div(me, NC), NY), lax.rem(me, NC)
    z_part = [lax.rem(z + step, NZ) * (NY * NC) for step in (4, 3, 5, 2, 6, 1, 7, 0)]

    def plane(i):
        return lax.rem(y + lax.div(i, NC), NY) * NC + lax.rem(c + lax.rem(i, NC), NC)

    own_plane = [z_part[-1] + plane(i) for i in range(1, NY * NC)]
    near = [part + y * NC + c for part in z_part[:-1]] + own_plane

    def far_peers(act):
        def others(i, carry):
            rest = plane(i)
            for part in z_part[:-1]:
                act(part + rest)
            return carry

        lax.fori_loop(1, NY * NC, others, 0)

    def load(n, src, dst):
        for j in range(LOCAL_HEADS):
            cols = pl.ds(j * HEAD_DIM, HEAD_DIM)
            pltpu.make_async_copy(src.at[:, cols], dst.at[j], in_sem.at[n]).start()

    def loaded(n, dst):
        pltpu.make_async_copy(dst, dst, in_sem.at[n]).wait()

    def arrived(got, sem):
        pltpu.make_async_copy(got, got, sem).wait()

    def by_place(act):
        def one_plane(k, carry):
            for i in range(NY * NC):
                other = k * (NY * NC) + plane(i)
                pl.when(other != me)(functools.partial(act, other))
            return carry

        lax.fori_loop(0, NZ, one_plane, 0)

    def near_first(act, between=lambda: None):
        for other in near:
            act(other)
        between()
        far_peers(act)

    def send_all(src, dst, mine, send_sem, recv_sem, order=near_first):
        pltpu.make_async_copy(src(me), mine, recv_sem).start()

        def send(other):
            pltpu.make_async_remote_copy(
                src_ref=src(other),
                dst_ref=dst,
                send_sem=send_sem,
                recv_sem=recv_sem,
                device_id=(other, head),
                device_id_type=MESH,
            ).start()

        order(send)

    smalls = [
        pltpu.make_async_copy(src, dst, small_sem.at[n])
        for n, (src, dst) in enumerate(
            ((head_class_hbm, head_class), (mask_s_hbm, mask_s), (mask_t_hbm, mask_t))
        )
    ]
    smalls[0].start()
    load(1, k_hbm, k_all)

    barrier = pltpu.get_barrier_semaphore()
    for other in near:
        pl.semaphore_signal(barrier, inc=1, device_id=(other, head), device_id_type=MESH)
    for small in smalls[1:]:
        small.start()
    smalls[0].wait()

    ranks, count_t, count_s = [], jnp.int32(0), jnp.int32(HT_DEV)
    for j in range(LOCAL_HEADS):
        is_t = head_class[j] > 0
        ranks.append(jnp.where(is_t, count_t, count_s))
        count_t = count_t + jnp.where(is_t, 1, 0)
        count_s = count_s + jnp.where(is_t, 0, 1)

    def head_of(n):
        place = jnp.int32(0)
        for j, rank in enumerate(ranks):
            place = jnp.where(rank == n, j, place)
        return place

    places = [head_of(t) for t in range(HT_DEV)]

    pl.semaphore_wait(barrier, len(near))
    for other in own_plane:
        pl.semaphore_signal(plane_sem, inc=1, device_id=(other, head), device_id_type=MESH)

    loaded(1, k_all)
    for t, place in enumerate(places):
        k_pack[:, t] = k_all[place].reshape(SEQ, PIECE, HEAD_DIM)
    send_all(
        lambda s: k_pack.at[s], k_got.at[me], k_got.at[me], kv_send_sem.at[0], kv_recv_sem.at[0],
        functools.partial(
            near_first, between=lambda: pl.semaphore_wait(plane_sem, len(own_plane))
        ),
    )
    load(2, v_hbm, v_all)
    load(0, q_hbm, q_all)
    loaded(2, v_all)
    for t, place in enumerate(places):
        v_pack[:, t] = v_all[place].reshape(SEQ, PIECE, HEAD_DIM)
    send_all(
        lambda s: v_pack.at[s], v_got.at[me], v_got.at[me], kv_send_sem.at[1], kv_recv_sem.at[1]
    )
    loaded(0, q_all)
    for t, place in enumerate(places):
        q_pack[t] = q_all[place].reshape(SEQ, PIECE, HEAD_DIM)

    def send_queries(t, carry):
        send_all(
            lambda s: q_pack.at[t, s], q_got.at[t, me], q_got.at[t, me],
            q_send_sem.at[t], q_recv_sem.at[t],
        )
        return carry

    lax.fori_loop(0, HT_DEV, send_queries, 0)

    for small in smalls[1:]:
        small.wait()
    row = lax.broadcasted_iota(jnp.int32, (TILE, TILE), 0) % PIECE // 2
    col = lax.broadcasted_iota(jnp.int32, (TILE, TILE), 1) % PIECE // 2
    bias = jnp.full((TILE, TILE), NEG, jnp.float32)
    for g in range(mask_t.shape[2]):
        for i in range(2):
            for j in range(2):
                value = jnp.where(mask_t[i, j, g] > 0, 0.0, NEG).astype(jnp.float32)
                bias = jnp.where((row == 2 * g + i) & (col == 2 * g + j), value, bias)
    t_bias[...] = bias

    def spatial_head(n, carry):
        place = head_of(HT_DEV + n)

        def block(r, inner):
            at = pl.multiple_of(r * STEP, STEP)

            def tile_bias(a, b):
                allowed = mask_s[0, r * (STEP // TILE) + a, b] > 0
                return jnp.where(allowed, 0.0, NEG).astype(jnp.float32)

            out[HT_DEV + n, pl.ds(at, STEP)] = attend_rows(
                q_all[place, pl.ds(at, STEP)], k_all[place], v_all[place], tile_bias
            )
            return inner

        lax.fori_loop(0, ROWS // STEP, block, 0)
        return carry

    lax.fori_loop(0, HS_DEV, spatial_head, 0)

    arrived(k_got, kv_recv_sem.at[0])
    arrived(v_got, kv_recv_sem.at[1])

    def temporal_head(t, carry):
        arrived(q_got.at[t], q_recv_sem.at[t])

        def block(r, inner):
            frames = STEP // PIECE
            at = pl.ds(r * frames, frames)
            mixed = attend_rows(
                q_got[t, at].reshape(STEP, HEAD_DIM),
                k_got[:, t].reshape(ROWS, HEAD_DIM),
                v_got[:, t].reshape(ROWS, HEAD_DIM),
                lambda a, b: t_bias[...],
            )
            o_send[t, at] = mixed.reshape(frames, PIECE, HEAD_DIM)
            return inner

        lax.fori_loop(0, ROWS // STEP, block, 0)
        mine = out.at[t, pl.ds(pl.multiple_of(me * PIECE, PIECE), PIECE)]
        send_all(
            lambda s: o_send.at[t, s], mine, mine, o_send_sem.at[t], o_recv_sem.at[t], by_place
        )
        return carry

    lax.fori_loop(0, HT_DEV, temporal_head, 0)

    others = pl.ds(0, SEQ - 1)
    arrived(k_pack.at[others], kv_send_sem.at[0])
    arrived(v_pack.at[others], kv_send_sem.at[1])

    def finish(t, carry):
        arrived(q_pack.at[t, others], q_send_sem.at[t])
        arrived(o_send.at[t, others], o_send_sem.at[t])
        arrived(out.at[t], o_recv_sem.at[t])
        return carry

    lax.fori_loop(0, HT_DEV, finish, 0)


def place_kernel(head_class, packed, out, sem):
    count_t, count_s = jnp.int32(0), jnp.int32(HT_DEV)
    copies = []
    for j in range(LOCAL_HEADS):
        is_t = head_class[j] > 0
        rank = jnp.where(is_t, count_t, count_s)
        count_t = count_t + jnp.where(is_t, 1, 0)
        count_s = count_s + jnp.where(is_t, 0, 1)
        copy = pltpu.make_async_copy(
            packed.at[rank], out.at[:, pl.ds(j * HEAD_DIM, HEAD_DIM)], sem.at[j]
        )
        copy.start()
        copies.append(copy)
    for copy in copies:
        copy.wait()


def on_device(queries, keys, values, head_class, mask_spatial, mask_temporal):
    smem = pl.BlockSpec(memory_space=pltpu.SMEM)
    anywhere = pl.BlockSpec(memory_space=pl.ANY)
    whole = pltpu.VMEM((LOCAL_HEADS, ROWS, HEAD_DIM), jnp.bfloat16)
    by_device = pltpu.VMEM((SEQ, HT_DEV, PIECE, HEAD_DIM), jnp.bfloat16)
    by_head = pltpu.VMEM((HT_DEV, SEQ, PIECE, HEAD_DIM), jnp.bfloat16)
    packed = pl.pallas_call(
        main_kernel,
        out_shape=pltpu.VMEM((LOCAL_HEADS, ROWS, HEAD_DIM), jnp.bfloat16),
        in_specs=[anywhere] * 6,
        out_specs=pl.BlockSpec(memory_space=pltpu.VMEM),
        scratch_shapes=[
            pltpu.SMEM(head_class.shape, jnp.int32),
            pltpu.SMEM(mask_spatial.shape, jnp.int32),
            pltpu.SMEM(mask_temporal.shape[1:] + mask_temporal.shape[:1], jnp.int32),
            whole, whole, whole,
            by_device, by_device, by_head, by_device, by_device, by_head, by_head,
            pltpu.VMEM((TILE, TILE), jnp.float32),
            pltpu.SemaphoreType.DMA((3,)),
            pltpu.SemaphoreType.DMA((3,)),
            pltpu.SemaphoreType.REGULAR,
            pltpu.SemaphoreType.DMA((2,)),
            pltpu.SemaphoreType.DMA((2,)),
            pltpu.SemaphoreType.DMA((HT_DEV,)),
            pltpu.SemaphoreType.DMA((HT_DEV,)),
            pltpu.SemaphoreType.DMA((HT_DEV,)),
            pltpu.SemaphoreType.DMA((HT_DEV,)),
        ],
        compiler_params=pltpu.CompilerParams(
            collective_id=0, has_side_effects=True, vmem_limit_bytes=60 << 20
        ),
        cost_estimate=pl.CostEstimate(
            flops=10 * 4 * ROWS * ROWS * HEAD_DIM,
            bytes_accessed=10 << 20,
            transcendentals=10 * ROWS * ROWS,
        ),
        name="attend_and_move",
    )(head_class, mask_spatial, jnp.transpose(mask_temporal, (1, 2, 0)), queries, keys, values)
    return pl.pallas_call(
        place_kernel,
        out_shape=jax.ShapeDtypeStruct((ROWS, LOCAL_HEADS * HEAD_DIM), jnp.bfloat16),
        in_specs=[smem, anywhere],
        out_specs=anywhere,
        scratch_shapes=[pltpu.SemaphoreType.DMA((LOCAL_HEADS,))],
        compiler_params=pltpu.CompilerParams(vmem_limit_bytes=8 << 20),
        name="place_heads",
    )(head_class, pltpu.with_memory_space_constraint(packed, pltpu.VMEM))


def solution(mesh):
    return jax.shard_map(
        on_device,
        mesh=mesh,
        in_specs=(
            P("seq", "head"),
            P("seq", "head"),
            P("seq", "head"),
            P("head"),
            P("seq", None, None),
            P("seq", None, None),
        ),
        out_specs=P("seq", "head"),
        check_vma=False,
    )
```

```python
import functools
import math

import jax
import jax.numpy as jnp
from jax import lax
from jax.experimental import pallas as pl
from jax.experimental.pallas import tpu as pltpu
from jax.sharding import PartitionSpec as P

HEAD_DIM = 128
TILE = 128
LOCAL_HEADS = 10
HT_DEV = 4
HS_DEV = LOCAL_HEADS - HT_DEV
ROWS = 1024
SEQ = 64
PIECE = ROWS // SEQ
NZ, NY, NC = 8, 4, 2
STEP = 256
EXP_SCALE = HEAD_DIM**-0.5 * math.log2(math.e)
NEG = -1e30
MESH = pl.DeviceIdType.MESH


def attend_rows(query, key_rows, value_rows, bias):
    scores = lax.dot_general(
        query, key_rows, (((1,), (1,)), ((), ())), preferred_element_type=jnp.float32
    )
    lows, totals = [], []
    for a in range(STEP // TILE):
        row = [
            scores[a * TILE : (a + 1) * TILE, b * TILE : (b + 1) * TILE] + bias(a, b)
            for b in range(ROWS // TILE)
        ]
        top = jnp.max(functools.reduce(jnp.maximum, row), axis=1, keepdims=True)
        weights = [jnp.exp2((part - top) * EXP_SCALE) for part in row]
        totals.append(jnp.sum(functools.reduce(jnp.add, weights), axis=1, keepdims=True))
        lows.append(jnp.concatenate([w.astype(jnp.bfloat16) for w in weights], axis=1))
    low = jnp.concatenate(lows, axis=0)
    total = jnp.concatenate(totals, axis=0)
    mixed = jnp.dot(low, value_rows, preferred_element_type=jnp.float32)
    return (mixed / total).astype(jnp.bfloat16)


def main_kernel(
    head_class_hbm, mask_s_hbm, mask_t_hbm, q_hbm, k_hbm, v_hbm, out,
    head_class, mask_s, mask_t, q_all, k_all, v_all, k_pack, v_pack, q_pack, k_got, v_got, q_got, o_send, t_bias,
    small_sem, in_sem, plane_sem, kv_send_sem, kv_recv_sem, q_send_sem, q_recv_sem, o_send_sem, o_recv_sem,
):
    me = lax.axis_index("seq")
    head = lax.axis_index("head")
    z, y, c = lax.div(me, NY * NC), lax.rem(lax.div(me, NC), NY), lax.rem(me, NC)
    z_part = [lax.rem(z + step, NZ) * (NY * NC) for step in (4, 3, 5, 2, 6, 1, 7, 0)]

    def plane(i):
        return lax.rem(y + lax.div(i, NC), NY) * NC + lax.rem(c + lax.rem(i, NC), NC)

    own_plane = [z_part[-1] + plane(i) for i in range(1, NY * NC)]
    near = [part + y * NC + c for part in z_part[:-1]] + own_plane

    def far_peers(act):
        def others(i, carry):
            rest = plane(i)
            for part in z_part[:-1]:
                act(part + rest)
            return carry

        lax.fori_loop(1, NY * NC, others, 0)

    def load(n, src, dst):
        for j in range(LOCAL_HEADS):
            cols = pl.ds(j * HEAD_DIM, HEAD_DIM)
            pltpu.make_async_copy(src.at[:, cols], dst.at[j], in_sem.at[n]).start()

    def loaded(n, dst):
        pltpu.make_async_copy(dst, dst, in_sem.at[n]).wait()

    def arrived(got, sem):
        pltpu.make_async_copy(got, got, sem).wait()

    def by_index(act):
        def one_plane(k, carry):
            for i in range(NY * NC):
                other = k * (NY * NC) + i
                pl.when(other != me)(functools.partial(act, other))
            return carry

        lax.fori_loop(0, NZ, one_plane, 0)

    def near_first(act, between=lambda: None):
        for other in near:
            act(other)
        between()
        far_peers(act)

    def send_all(src, dst, mine, send_sem, recv_sem, order=near_first):
        pltpu.make_async_copy(src(me), mine, recv_sem).start()

        def send(other):
            pltpu.make_async_remote_copy(
                src_ref=src(other),
                dst_ref=dst,
                send_sem=send_sem,
                recv_sem=recv_sem,
                device_id=(other, head),
                device_id_type=MESH,
            ).start()

        order(send)

    smalls = [
        pltpu.make_async_copy(src, dst, small_sem.at[n])
        for n, (src, dst) in enumerate(
            ((head_class_hbm, head_class), (mask_s_hbm, mask_s), (mask_t_hbm, mask_t))
        )
    ]
    smalls[0].start()
    load(1, k_hbm, k_all)

    barrier = pltpu.get_barrier_semaphore()
    for other in near:
        pl.semaphore_signal(barrier, inc=1, device_id=(other, head), device_id_type=MESH)
    for small in smalls[1:]:
        small.start()
    smalls[0].wait()

    ranks, count_t, count_s = [], jnp.int32(0), jnp.int32(HT_DEV)
    for j in range(LOCAL_HEADS):
        is_t = head_class[j] > 0
        ranks.append(jnp.where(is_t, count_t, count_s))
        count_t = count_t + jnp.where(is_t, 1, 0)
        count_s = count_s + jnp.where(is_t, 0, 1)

    def head_of(n):
        place = jnp.int32(0)
        for j, rank in enumerate(ranks):
            place = jnp.where(rank == n, j, place)
        return place

    places = [head_of(t) for t in range(HT_DEV)]

    pl.semaphore_wait(barrier, len(near))
    for other in own_plane:
        pl.semaphore_signal(plane_sem, inc=1, device_id=(other, head), device_id_type=MESH)

    loaded(1, k_all)
    for t, place in enumerate(places):
        k_pack[:, t] = k_all[place].reshape(SEQ, PIECE, HEAD_DIM)
    send_all(
        lambda s: k_pack.at[s], k_got.at[me], k_got.at[me], kv_send_sem.at[0], kv_recv_sem.at[0],
        functools.partial(
            near_first, between=lambda: pl.semaphore_wait(plane_sem, len(own_plane))
        ),
    )
    load(2, v_hbm, v_all)
    load(0, q_hbm, q_all)
    loaded(2, v_all)
    for t, place in enumerate(places):
        v_pack[:, t] = v_all[place].reshape(SEQ, PIECE, HEAD_DIM)
    send_all(
        lambda s: v_pack.at[s], v_got.at[me], v_got.at[me], kv_send_sem.at[1], kv_recv_sem.at[1]
    )
    loaded(0, q_all)
    for t, place in enumerate(places):
        q_pack[t] = q_all[place].reshape(SEQ, PIECE, HEAD_DIM)

    def send_queries(t, carry):
        send_all(
            lambda s: q_pack.at[t, s], q_got.at[t, me], q_got.at[t, me],
            q_send_sem.at[t], q_recv_sem.at[t],
        )
        return carry

    lax.fori_loop(0, HT_DEV, send_queries, 0)

    for small in smalls[1:]:
        small.wait()
    row = lax.broadcasted_iota(jnp.int32, (TILE, TILE), 0) % PIECE // 2
    col = lax.broadcasted_iota(jnp.int32, (TILE, TILE), 1) % PIECE // 2
    bias = jnp.full((TILE, TILE), NEG, jnp.float32)
    for g in range(mask_t.shape[2]):
        for i in range(2):
            for j in range(2):
                value = jnp.where(mask_t[i, j, g] > 0, 0.0, NEG).astype(jnp.float32)
                bias = jnp.where((row == 2 * g + i) & (col == 2 * g + j), value, bias)
    t_bias[...] = bias

    def spatial_head(n, carry):
        place = head_of(HT_DEV + n)

        def block(r, inner):
            at = pl.multiple_of(r * STEP, STEP)

            def tile_bias(a, b):
                allowed = mask_s[0, r * (STEP // TILE) + a, b] > 0
                return jnp.where(allowed, 0.0, NEG).astype(jnp.float32)

            out[HT_DEV + n, pl.ds(at, STEP)] = attend_rows(
                q_all[place, pl.ds(at, STEP)], k_all[place], v_all[place], tile_bias
            )
            return inner

        lax.fori_loop(0, ROWS // STEP, block, 0)
        return carry

    lax.fori_loop(0, HS_DEV, spatial_head, 0)

    arrived(k_got, kv_recv_sem.at[0])
    arrived(v_got, kv_recv_sem.at[1])

    def temporal_head(t, carry):
        arrived(q_got.at[t], q_recv_sem.at[t])

        def block(r, inner):
            frames = STEP // PIECE
            at = pl.ds(r * frames, frames)
            mixed = attend_rows(
                q_got[t, at].reshape(STEP, HEAD_DIM),
                k_got[:, t].reshape(ROWS, HEAD_DIM),
                v_got[:, t].reshape(ROWS, HEAD_DIM),
                lambda a, b: t_bias[...],
            )
            o_send[t, at] = mixed.reshape(frames, PIECE, HEAD_DIM)
            return inner

        lax.fori_loop(0, ROWS // STEP, block, 0)
        mine = out.at[t, pl.ds(pl.multiple_of(me * PIECE, PIECE), PIECE)]
        send_all(
            lambda s: o_send.at[t, s], mine, mine, o_send_sem.at[t], o_recv_sem.at[t], by_index
        )
        return carry

    lax.fori_loop(0, HT_DEV, temporal_head, 0)

    others = pl.ds(0, SEQ - 1)
    arrived(k_pack.at[others], kv_send_sem.at[0])
    arrived(v_pack.at[others], kv_send_sem.at[1])

    def finish(t, carry):
        arrived(q_pack.at[t, others], q_send_sem.at[t])
        arrived(o_send.at[t, others], o_send_sem.at[t])
        arrived(out.at[t], o_recv_sem.at[t])
        return carry

    lax.fori_loop(0, HT_DEV, finish, 0)


def place_kernel(head_class, packed, out, sem):
    count_t, count_s = jnp.int32(0), jnp.int32(HT_DEV)
    copies = []
    for j in range(LOCAL_HEADS):
        is_t = head_class[j] > 0
        rank = jnp.where(is_t, count_t, count_s)
        count_t = count_t + jnp.where(is_t, 1, 0)
        count_s = count_s + jnp.where(is_t, 0, 1)
        copy = pltpu.make_async_copy(
            packed.at[rank], out.at[:, pl.ds(j * HEAD_DIM, HEAD_DIM)], sem.at[j]
        )
        copy.start()
        copies.append(copy)
    for copy in copies:
        copy.wait()


def on_device(queries, keys, values, head_class, mask_spatial, mask_temporal):
    smem = pl.BlockSpec(memory_space=pltpu.SMEM)
    anywhere = pl.BlockSpec(memory_space=pl.ANY)
    whole = pltpu.VMEM((LOCAL_HEADS, ROWS, HEAD_DIM), jnp.bfloat16)
    by_device = pltpu.VMEM((SEQ, HT_DEV, PIECE, HEAD_DIM), jnp.bfloat16)
    by_head = pltpu.VMEM((HT_DEV, SEQ, PIECE, HEAD_DIM), jnp.bfloat16)
    packed = pl.pallas_call(
        main_kernel,
        out_shape=pltpu.VMEM((LOCAL_HEADS, ROWS, HEAD_DIM), jnp.bfloat16),
        in_specs=[anywhere] * 6,
        out_specs=pl.BlockSpec(memory_space=pltpu.VMEM),
        scratch_shapes=[
            pltpu.SMEM(head_class.shape, jnp.int32),
            pltpu.SMEM(mask_spatial.shape, jnp.int32),
            pltpu.SMEM(mask_temporal.shape[1:] + mask_temporal.shape[:1], jnp.int32),
            whole, whole, whole,
            by_device, by_device, by_head, by_device, by_device, by_head, by_head,
            pltpu.VMEM((TILE, TILE), jnp.float32),
            pltpu.SemaphoreType.DMA((3,)),
            pltpu.SemaphoreType.DMA((3,)),
            pltpu.SemaphoreType.REGULAR,
            pltpu.SemaphoreType.DMA((2,)),
            pltpu.SemaphoreType.DMA((2,)),
            pltpu.SemaphoreType.DMA((HT_DEV,)),
            pltpu.SemaphoreType.DMA((HT_DEV,)),
            pltpu.SemaphoreType.DMA((HT_DEV,)),
            pltpu.SemaphoreType.DMA((HT_DEV,)),
        ],
        compiler_params=pltpu.CompilerParams(
            collective_id=0, has_side_effects=True, vmem_limit_bytes=60 << 20
        ),
        cost_estimate=pl.CostEstimate(
            flops=10 * 4 * ROWS * ROWS * HEAD_DIM,
            bytes_accessed=10 << 20,
            transcendentals=10 * ROWS * ROWS,
        ),
        name="attend_and_move",
    )(head_class, mask_spatial, jnp.transpose(mask_temporal, (1, 2, 0)), queries, keys, values)
    return pl.pallas_call(
        place_kernel,
        out_shape=jax.ShapeDtypeStruct((ROWS, LOCAL_HEADS * HEAD_DIM), jnp.bfloat16),
        in_specs=[smem, anywhere],
        out_specs=anywhere,
        scratch_shapes=[pltpu.SemaphoreType.DMA((LOCAL_HEADS,))],
        compiler_params=pltpu.CompilerParams(vmem_limit_bytes=8 << 20),
        name="place_heads",
    )(head_class, pltpu.with_memory_space_constraint(packed, pltpu.VMEM))


def solution(mesh):
    return jax.shard_map(
        on_device,
        mesh=mesh,
        in_specs=(
            P("seq", "head"),
            P("seq", "head"),
            P("seq", "head"),
            P("head"),
            P("seq", None, None),
            P("seq", None, None),
        ),
        out_specs=P("seq", "head"),
        check_vma=False,
    )
```

```python
import functools
import math

import jax
import jax.numpy as jnp
from jax import lax
from jax.experimental import pallas as pl
from jax.experimental.pallas import tpu as pltpu
from jax.sharding import PartitionSpec as P

HEAD_DIM = 128
TILE = 128
LOCAL_HEADS = 10
HT_DEV = 4
HS_DEV = LOCAL_HEADS - HT_DEV
ROWS = 1024
SEQ = 64
PIECE = ROWS // SEQ
NZ, NY, NC = 8, 4, 2
PLANE = ROWS // NZ
STEP = 256
EXP_SCALE = HEAD_DIM**-0.5 * math.log2(math.e)
NEG = -1e30
MESH = pl.DeviceIdType.MESH


def attend_rows(query, key_rows, value_rows, bias):
    scores = lax.dot_general(
        query, key_rows, (((1,), (1,)), ((), ())), preferred_element_type=jnp.float32
    )
    lows, totals = [], []
    for a in range(STEP // TILE):
        row = [
            scores[a * TILE : (a + 1) * TILE, b * TILE : (b + 1) * TILE] + bias(a, b)
            for b in range(ROWS // TILE)
        ]
        top = jnp.max(functools.reduce(jnp.maximum, row), axis=1, keepdims=True)
        weights = [jnp.exp2((part - top) * EXP_SCALE) for part in row]
        totals.append(jnp.sum(functools.reduce(jnp.add, weights), axis=1, keepdims=True))
        lows.append(jnp.concatenate([w.astype(jnp.bfloat16) for w in weights], axis=1))
    low = jnp.concatenate(lows, axis=0)
    total = jnp.concatenate(totals, axis=0)
    mixed = jnp.dot(low, value_rows, preferred_element_type=jnp.float32)
    return (mixed / total).astype(jnp.bfloat16)


def main_kernel(
    head_class_hbm, mask_s_hbm, mask_t_hbm, q_hbm, k_hbm, v_hbm, out,
    head_class, mask_s, mask_t, q_all, k_all, v_all, k_pack, v_pack, q_pack, k_got, v_got, q_got, o_send, s_done, t_done, t_bias,
    small_sem, in_sem, plane_sem, kv_send_sem, kv_recv_sem, q_send_sem, q_recv_sem, o_send_sem, o_recv_sem,
):
    me = lax.axis_index("seq")
    head = lax.axis_index("head")
    z, y, c = lax.div(me, NY * NC), lax.rem(lax.div(me, NC), NY), lax.rem(me, NC)
    z_part = [lax.rem(z + step, NZ) * (NY * NC) for step in (4, 3, 5, 2, 6, 1, 7, 0)]

    def plane(i):
        return lax.rem(y + lax.div(i, NC), NY) * NC + lax.rem(c + lax.rem(i, NC), NC)

    own_plane = [z_part[-1] + plane(i) for i in range(1, NY * NC)]
    near = [part + y * NC + c for part in z_part[:-1]] + own_plane

    def far_peers(act):
        def others(i, carry):
            rest = plane(i)
            for part in z_part[:-1]:
                act(part + rest)
            return carry

        lax.fori_loop(1, NY * NC, others, 0)

    def load(n, src, dst):
        for j in range(LOCAL_HEADS):
            cols = pl.ds(j * HEAD_DIM, HEAD_DIM)
            pltpu.make_async_copy(src.at[:, cols], dst.at[j], in_sem.at[n]).start()

    def loaded(n, dst):
        pltpu.make_async_copy(dst, dst, in_sem.at[n]).wait()

    def arrived(got, sem):
        pltpu.make_async_copy(got, got, sem).wait()

    def by_index(act):
        def one_plane(k, carry):
            for i in range(NY * NC):
                other = k * (NY * NC) + i
                pl.when(other != me)(functools.partial(act, other))
            return carry

        lax.fori_loop(0, NZ, one_plane, 0)

    def near_first(act, between=lambda: None):
        for other in near:
            act(other)
        between()
        far_peers(act)

    def send_all(src, dst, mine, send_sem, recv_sem, order=near_first):
        pltpu.make_async_copy(src(me), mine, recv_sem).start()

        def send(other):
            pltpu.make_async_remote_copy(
                src_ref=src(other),
                dst_ref=dst,
                send_sem=send_sem,
                recv_sem=recv_sem,
                device_id=(other, head),
                device_id_type=MESH,
            ).start()

        order(send)

    smalls = [
        pltpu.make_async_copy(src, dst, small_sem.at[n])
        for n, (src, dst) in enumerate(
            ((head_class_hbm, head_class), (mask_s_hbm, mask_s), (mask_t_hbm, mask_t))
        )
    ]
    smalls[0].start()
    load(1, k_hbm, k_all)

    barrier = pltpu.get_barrier_semaphore()
    for other in near:
        pl.semaphore_signal(barrier, inc=1, device_id=(other, head), device_id_type=MESH)
    for small in smalls[1:]:
        small.start()
    smalls[0].wait()

    ranks, count_t, count_s = [], jnp.int32(0), jnp.int32(HT_DEV)
    for j in range(LOCAL_HEADS):
        is_t = head_class[j] > 0
        ranks.append(jnp.where(is_t, count_t, count_s))
        count_t = count_t + jnp.where(is_t, 1, 0)
        count_s = count_s + jnp.where(is_t, 0, 1)

    def head_of(n):
        place = jnp.int32(0)
        for j, rank in enumerate(ranks):
            place = jnp.where(rank == n, j, place)
        return place

    places = [head_of(t) for t in range(HT_DEV)]

    pl.semaphore_wait(barrier, len(near))
    for other in own_plane:
        pl.semaphore_signal(plane_sem, inc=1, device_id=(other, head), device_id_type=MESH)

    loaded(1, k_all)
    for t, place in enumerate(places):
        k_pack[:, t] = k_all[place].reshape(SEQ, PIECE, HEAD_DIM)
    send_all(
        lambda s: k_pack.at[s], k_got.at[me], k_got.at[me], kv_send_sem.at[0], kv_recv_sem.at[0],
        functools.partial(
            near_first, between=lambda: pl.semaphore_wait(plane_sem, len(own_plane))
        ),
    )
    load(2, v_hbm, v_all)
    load(0, q_hbm, q_all)
    loaded(2, v_all)
    for t, place in enumerate(places):
        v_pack[:, t] = v_all[place].reshape(SEQ, PIECE, HEAD_DIM)
    send_all(
        lambda s: v_pack.at[s], v_got.at[me], v_got.at[me], kv_send_sem.at[1], kv_recv_sem.at[1]
    )
    loaded(0, q_all)
    for t, place in enumerate(places):
        q_pack[t] = q_all[place].reshape(SEQ, PIECE, HEAD_DIM)

    def send_queries(t, carry):
        send_all(
            lambda s: q_pack.at[t, s], q_got.at[t, me], q_got.at[t, me],
            q_send_sem.at[t], q_recv_sem.at[t],
        )
        return carry

    lax.fori_loop(0, HT_DEV, send_queries, 0)

    for small in smalls[1:]:
        small.wait()
    row = lax.broadcasted_iota(jnp.int32, (TILE, TILE), 0) % PIECE // 2
    col = lax.broadcasted_iota(jnp.int32, (TILE, TILE), 1) % PIECE // 2
    bias = jnp.full((TILE, TILE), NEG, jnp.float32)
    for g in range(mask_t.shape[2]):
        for i in range(2):
            for j in range(2):
                value = jnp.where(mask_t[i, j, g] > 0, 0.0, NEG).astype(jnp.float32)
                bias = jnp.where((row == 2 * g + i) & (col == 2 * g + j), value, bias)
    t_bias[...] = bias

    def spatial_head(n, carry):
        place = head_of(HT_DEV + n)

        def block(r, inner):
            at = pl.multiple_of(r * STEP, STEP)

            def tile_bias(a, b):
                allowed = mask_s[0, r * (STEP // TILE) + a, b] > 0
                return jnp.where(allowed, 0.0, NEG).astype(jnp.float32)

            s_done[n, pl.ds(at, STEP)] = attend_rows(
                q_all[place, pl.ds(at, STEP)], k_all[place], v_all[place], tile_bias
            )
            return inner

        lax.fori_loop(0, ROWS // STEP, block, 0)
        return carry

    lax.fori_loop(0, HS_DEV, spatial_head, 0)
    for j, rank in enumerate(ranks):
        out[:, j * HEAD_DIM : (j + 1) * HEAD_DIM] = s_done[jnp.clip(rank - HT_DEV, 0, HS_DEV - 1)]

    arrived(k_got, kv_recv_sem.at[0])
    arrived(v_got, kv_recv_sem.at[1])

    def temporal_head(t, carry):
        arrived(q_got.at[t], q_recv_sem.at[t])

        def block(r, inner):
            frames = STEP // PIECE
            at = pl.ds(r * frames, frames)
            mixed = attend_rows(
                q_got[t, at].reshape(STEP, HEAD_DIM),
                k_got[:, t].reshape(ROWS, HEAD_DIM),
                v_got[:, t].reshape(ROWS, HEAD_DIM),
                lambda a, b: t_bias[...],
            )
            o_send[t, at] = mixed.reshape(frames, PIECE, HEAD_DIM)
            return inner

        lax.fori_loop(0, ROWS // STEP, block, 0)
        mine = t_done.at[t, pl.ds(pl.multiple_of(me * PIECE, PIECE), PIECE)]
        send_all(
            lambda s: o_send.at[t, s], mine, mine, o_send_sem.at[t], o_recv_sem.at[t, z], by_index
        )
        return carry

    lax.fori_loop(0, HT_DEV, temporal_head, 0)

    others = pl.ds(0, SEQ - 1)
    arrived(k_pack.at[others], kv_send_sem.at[0])
    arrived(v_pack.at[others], kv_send_sem.at[1])

    def place(t):
        def one_plane(i, carry):
            step = (1 - 2 * lax.rem(i, 2)) * lax.div(i + 1, 2)
            k = lax.rem(z + NZ + step, NZ)
            at = pl.ds(pl.multiple_of(k * PLANE, PLANE), PLANE)
            arrived(t_done.at[t, at], o_recv_sem.at[t, k])
            for j in range(t, t + HS_DEV + 1):
                cols = pl.ds(j * HEAD_DIM, HEAD_DIM)
                out[at, cols] = jnp.where(ranks[j] == t, t_done[t, at], out[at, cols])
            return carry

        lax.fori_loop(0, NZ, one_plane, 0)

    for t in range(HT_DEV):
        arrived(q_pack.at[t, others], q_send_sem.at[t])
        place(t)
        arrived(o_send.at[t, others], o_send_sem.at[t])


def on_device(queries, keys, values, head_class, mask_spatial, mask_temporal):
    smem = pl.BlockSpec(memory_space=pltpu.SMEM)
    anywhere = pl.BlockSpec(memory_space=pl.ANY)
    whole = pltpu.VMEM((LOCAL_HEADS, ROWS, HEAD_DIM), jnp.bfloat16)
    by_device = pltpu.VMEM((SEQ, HT_DEV, PIECE, HEAD_DIM), jnp.bfloat16)
    by_head = pltpu.VMEM((HT_DEV, SEQ, PIECE, HEAD_DIM), jnp.bfloat16)
    return pl.pallas_call(
        main_kernel,
        out_shape=pltpu.VMEM((ROWS, LOCAL_HEADS * HEAD_DIM), jnp.bfloat16),
        in_specs=[anywhere] * 6,
        out_specs=pl.BlockSpec(memory_space=pltpu.VMEM),
        scratch_shapes=[
            pltpu.SMEM(head_class.shape, jnp.int32),
            pltpu.SMEM(mask_spatial.shape, jnp.int32),
            pltpu.SMEM(mask_temporal.shape[1:] + mask_temporal.shape[:1], jnp.int32),
            whole, whole, whole,
            by_device, by_device, by_head, by_device, by_device, by_head, by_head,
            pltpu.VMEM((HS_DEV, ROWS, HEAD_DIM), jnp.bfloat16),
            pltpu.VMEM((HT_DEV, ROWS, HEAD_DIM), jnp.bfloat16),
            pltpu.VMEM((TILE, TILE), jnp.float32),
            pltpu.SemaphoreType.DMA((3,)),
            pltpu.SemaphoreType.DMA((3,)),
            pltpu.SemaphoreType.REGULAR,
            pltpu.SemaphoreType.DMA((2,)),
            pltpu.SemaphoreType.DMA((2,)),
            pltpu.SemaphoreType.DMA((HT_DEV,)),
            pltpu.SemaphoreType.DMA((HT_DEV,)),
            pltpu.SemaphoreType.DMA((HT_DEV,)),
            pltpu.SemaphoreType.DMA((HT_DEV, NZ)),
        ],
        compiler_params=pltpu.CompilerParams(
            collective_id=0, has_side_effects=True, vmem_limit_bytes=60 << 20
        ),
        cost_estimate=pl.CostEstimate(
            flops=10 * 4 * ROWS * ROWS * HEAD_DIM,
            bytes_accessed=10 << 20,
            transcendentals=10 * ROWS * ROWS,
        ),
        name="attend_and_move",
    )(head_class, mask_spatial, jnp.transpose(mask_temporal, (1, 2, 0)), queries, keys, values)


def solution(mesh):
    return jax.shard_map(
        on_device,
        mesh=mesh,
        in_specs=(
            P("seq", "head"),
            P("seq", "head"),
            P("seq", "head"),
            P("head"),
            P("seq", None, None),
            P("seq", None, None),
        ),
        out_specs=P("seq", "head"),
        check_vma=False,
    )
```

```python
import functools
import math

import jax
import jax.numpy as jnp
from jax import lax
from jax.experimental import pallas as pl
from jax.experimental.pallas import tpu as pltpu
from jax.sharding import PartitionSpec as P

HEAD_DIM = 128
TILE = 128
LOCAL_HEADS = 10
HT_DEV = 4
HS_DEV = LOCAL_HEADS - HT_DEV
ROWS = 1024
SEQ = 64
PIECE = ROWS // SEQ
NZ, NY, NC = 8, 4, 2
STEP = 256
EXP_SCALE = HEAD_DIM**-0.5 * math.log2(math.e)
NEG = -1e30
MESH = pl.DeviceIdType.MESH


def attend_rows(query, key_rows, value_rows, bias):
    scores = lax.dot_general(
        query, key_rows, (((1,), (1,)), ((), ())), preferred_element_type=jnp.float32
    )
    lows, totals = [], []
    for a in range(STEP // TILE):
        row = [
            scores[a * TILE : (a + 1) * TILE, b * TILE : (b + 1) * TILE] + bias(a, b)
            for b in range(ROWS // TILE)
        ]
        top = jnp.max(functools.reduce(jnp.maximum, row), axis=1, keepdims=True)
        weights = [jnp.exp2((part - top) * EXP_SCALE) for part in row]
        totals.append(jnp.sum(functools.reduce(jnp.add, weights), axis=1, keepdims=True))
        lows.append(jnp.concatenate([w.astype(jnp.bfloat16) for w in weights], axis=1))
    low = jnp.concatenate(lows, axis=0)
    total = jnp.concatenate(totals, axis=0)
    mixed = jnp.dot(low, value_rows, preferred_element_type=jnp.float32)
    return (mixed / total).astype(jnp.bfloat16)


def main_kernel(
    head_class_hbm, mask_s_hbm, mask_t_hbm, q_hbm, k_hbm, v_hbm, out,
    head_class, mask_s, mask_t, q_all, k_all, v_all, k_pack, v_pack, q_pack, k_got, v_got, q_got, o_send, t_bias,
    small_sem, in_sem, plane_sem, kv_send_sem, kv_recv_sem, q_send_sem, q_recv_sem, o_send_sem, o_recv_sem,
):
    me = lax.axis_index("seq")
    head = lax.axis_index("head")
    z, y, c = lax.div(me, NY * NC), lax.rem(lax.div(me, NC), NY), lax.rem(me, NC)
    z_part = [lax.rem(z + step, NZ) * (NY * NC) for step in (4, 3, 5, 2, 6, 1, 7, 0)]

    def plane(i):
        return lax.rem(y + lax.div(i, NC), NY) * NC + lax.rem(c + lax.rem(i, NC), NC)

    own_plane = [z_part[-1] + plane(i) for i in range(1, NY * NC)]
    near = [part + y * NC + c for part in z_part[:-1]] + own_plane

    def far_peers(act):
        def others(i, carry):
            rest = plane(i)
            for part in z_part[:-1]:
                act(part + rest)
            return carry

        lax.fori_loop(1, NY * NC, others, 0)

    def load(n, src, dst):
        for j in range(LOCAL_HEADS):
            cols = pl.ds(j * HEAD_DIM, HEAD_DIM)
            pltpu.make_async_copy(src.at[:, cols], dst.at[j], in_sem.at[n]).start()

    def loaded(n, dst):
        pltpu.make_async_copy(dst, dst, in_sem.at[n]).wait()

    def arrived(got, sem):
        pltpu.make_async_copy(got, got, sem).wait()

    def by_index(act):
        def one_plane(k, carry):
            for i in range(NY * NC):
                other = k * (NY * NC) + i
                pl.when(other != me)(functools.partial(act, other))
            return carry

        lax.fori_loop(0, NZ, one_plane, 0)

    def near_first(act, between=lambda: None):
        for other in near:
            act(other)
        between()
        far_peers(act)

    def send_all(src, dst, mine, send_sem, recv_sem, order=near_first):
        pltpu.make_async_copy(src(me), mine, recv_sem).start()

        def send(other):
            pltpu.make_async_remote_copy(
                src_ref=src(other),
                dst_ref=dst,
                send_sem=send_sem,
                recv_sem=recv_sem,
                device_id=(other, head),
                device_id_type=MESH,
            ).start()

        order(send)

    smalls = [
        pltpu.make_async_copy(src, dst, small_sem.at[n])
        for n, (src, dst) in enumerate(
            ((head_class_hbm, head_class), (mask_s_hbm, mask_s), (mask_t_hbm, mask_t))
        )
    ]
    smalls[0].start()
    load(1, k_hbm, k_all)

    barrier = pltpu.get_barrier_semaphore()
    for other in near:
        pl.semaphore_signal(barrier, inc=1, device_id=(other, head), device_id_type=MESH)
    for small in smalls[1:]:
        small.start()
    smalls[0].wait()

    ranks, count_t, count_s = [], jnp.int32(0), jnp.int32(HT_DEV)
    for j in range(LOCAL_HEADS):
        is_t = head_class[j] > 0
        ranks.append(jnp.where(is_t, count_t, count_s))
        count_t = count_t + jnp.where(is_t, 1, 0)
        count_s = count_s + jnp.where(is_t, 0, 1)

    def head_of(n):
        place = jnp.int32(0)
        for j, rank in enumerate(ranks):
            place = jnp.where(rank == n, j, place)
        return place

    places = [head_of(t) for t in range(HT_DEV)]

    pl.semaphore_wait(barrier, len(near))
    for other in own_plane:
        pl.semaphore_signal(plane_sem, inc=1, device_id=(other, head), device_id_type=MESH)

    loaded(1, k_all)
    for t, place in enumerate(places):
        k_pack[:, t] = k_all[place].reshape(SEQ, PIECE, HEAD_DIM)
    send_all(
        lambda s: k_pack.at[s], k_got.at[me], k_got.at[me], kv_send_sem.at[0], kv_recv_sem.at[0],
        functools.partial(
            near_first, between=lambda: pl.semaphore_wait(plane_sem, len(own_plane))
        ),
    )
    load(2, v_hbm, v_all)
    load(0, q_hbm, q_all)
    loaded(2, v_all)
    for t, place in enumerate(places):
        v_pack[:, t] = v_all[place].reshape(SEQ, PIECE, HEAD_DIM)
    send_all(
        lambda s: v_pack.at[s], v_got.at[me], v_got.at[me], kv_send_sem.at[1], kv_recv_sem.at[1]
    )
    loaded(0, q_all)
    for t, place in enumerate(places):
        q_pack[t] = q_all[place].reshape(SEQ, PIECE, HEAD_DIM)

    def send_queries(t, carry):
        send_all(
            lambda s: q_pack.at[t, s], q_got.at[t, me], q_got.at[t, me],
            q_send_sem.at[t], q_recv_sem.at[t],
        )
        return carry

    lax.fori_loop(0, HT_DEV, send_queries, 0)

    for small in smalls[1:]:
        small.wait()
    row = lax.broadcasted_iota(jnp.int32, (TILE, TILE), 0) % PIECE // 2
    col = lax.broadcasted_iota(jnp.int32, (TILE, TILE), 1) % PIECE // 2
    bias = jnp.full((TILE, TILE), NEG, jnp.float32)
    for g in range(mask_t.shape[2]):
        for i in range(2):
            for j in range(2):
                value = jnp.where(mask_t[i, j, g] > 0, 0.0, NEG).astype(jnp.float32)
                bias = jnp.where((row == 2 * g + i) & (col == 2 * g + j), value, bias)
    t_bias[...] = bias

    def spatial_head(n, carry):
        place = head_of(HT_DEV + n)

        def block(r, inner):
            at = pl.multiple_of(r * STEP, STEP)

            def tile_bias(a, b):
                allowed = mask_s[0, r * (STEP // TILE) + a, b] > 0
                return jnp.where(allowed, 0.0, NEG).astype(jnp.float32)

            out[HT_DEV + n, pl.ds(at, STEP)] = attend_rows(
                q_all[place, pl.ds(at, STEP)], k_all[place], v_all[place], tile_bias
            )
            return inner

        lax.fori_loop(0, ROWS // STEP, block, 0)
        return carry

    lax.fori_loop(0, HS_DEV, spatial_head, 0)

    arrived(k_got, kv_recv_sem.at[0])
    arrived(v_got, kv_recv_sem.at[1])

    def temporal_head(t, carry):
        arrived(q_got.at[t], q_recv_sem.at[t])

        def block(r, inner):
            frames = STEP // PIECE
            at = pl.ds(r * frames, frames)
            mixed = attend_rows(
                q_got[t, at].reshape(STEP, HEAD_DIM),
                k_got[:, t].reshape(ROWS, HEAD_DIM),
                v_got[:, t].reshape(ROWS, HEAD_DIM),
                lambda a, b: t_bias[...],
            )
            o_send[t, at] = mixed.reshape(frames, PIECE, HEAD_DIM)
            return inner

        lax.fori_loop(0, ROWS // STEP, block, 0)
        return carry

    def return_heads(heads):
        at = pl.ds(pl.multiple_of(me * PIECE, PIECE), PIECE)
        for t in heads:
            pltpu.make_async_copy(o_send.at[t, me], out.at[t, at], o_recv_sem.at[t]).start()

        def send(other):
            for t in heads:
                pltpu.make_async_remote_copy(
                    src_ref=o_send.at[t, other],
                    dst_ref=out.at[t, at],
                    send_sem=o_send_sem.at[t],
                    recv_sem=o_recv_sem.at[t],
                    device_id=(other, head),
                    device_id_type=MESH,
                ).start()

        by_index(send)

    def early_head(t, carry):
        temporal_head(t, carry)
        return_heads((t,))
        return carry

    lax.fori_loop(0, HT_DEV - 2, early_head, 0)
    lax.fori_loop(HT_DEV - 2, HT_DEV, temporal_head, 0)
    return_heads((HT_DEV - 2, HT_DEV - 1))

    others = pl.ds(0, SEQ - 1)
    arrived(k_pack.at[others], kv_send_sem.at[0])
    arrived(v_pack.at[others], kv_send_sem.at[1])

    def finish(t, carry):
        arrived(q_pack.at[t, others], q_send_sem.at[t])
        arrived(o_send.at[t, others], o_send_sem.at[t])
        arrived(out.at[t], o_recv_sem.at[t])
        return carry

    lax.fori_loop(0, HT_DEV, finish, 0)


def place_kernel(head_class, packed, out, sem):
    count_t, count_s = jnp.int32(0), jnp.int32(HT_DEV)
    copies = []
    for j in range(LOCAL_HEADS):
        is_t = head_class[j] > 0
        rank = jnp.where(is_t, count_t, count_s)
        count_t = count_t + jnp.where(is_t, 1, 0)
        count_s = count_s + jnp.where(is_t, 0, 1)
        copy = pltpu.make_async_copy(
            packed.at[rank], out.at[:, pl.ds(j * HEAD_DIM, HEAD_DIM)], sem.at[j]
        )
        copy.start()
        copies.append(copy)
    for copy in copies:
        copy.wait()


def on_device(queries, keys, values, head_class, mask_spatial, mask_temporal):
    smem = pl.BlockSpec(memory_space=pltpu.SMEM)
    anywhere = pl.BlockSpec(memory_space=pl.ANY)
    whole = pltpu.VMEM((LOCAL_HEADS, ROWS, HEAD_DIM), jnp.bfloat16)
    by_device = pltpu.VMEM((SEQ, HT_DEV, PIECE, HEAD_DIM), jnp.bfloat16)
    by_head = pltpu.VMEM((HT_DEV, SEQ, PIECE, HEAD_DIM), jnp.bfloat16)
    packed = pl.pallas_call(
        main_kernel,
        out_shape=pltpu.VMEM((LOCAL_HEADS, ROWS, HEAD_DIM), jnp.bfloat16),
        in_specs=[anywhere] * 6,
        out_specs=pl.BlockSpec(memory_space=pltpu.VMEM),
        scratch_shapes=[
            pltpu.SMEM(head_class.shape, jnp.int32),
            pltpu.SMEM(mask_spatial.shape, jnp.int32),
            pltpu.SMEM(mask_temporal.shape[1:] + mask_temporal.shape[:1], jnp.int32),
            whole, whole, whole,
            by_device, by_device, by_head, by_device, by_device, by_head, by_head,
            pltpu.VMEM((TILE, TILE), jnp.float32),
            pltpu.SemaphoreType.DMA((3,)),
            pltpu.SemaphoreType.DMA((3,)),
            pltpu.SemaphoreType.REGULAR,
            pltpu.SemaphoreType.DMA((2,)),
            pltpu.SemaphoreType.DMA((2,)),
            pltpu.SemaphoreType.DMA((HT_DEV,)),
            pltpu.SemaphoreType.DMA((HT_DEV,)),
            pltpu.SemaphoreType.DMA((HT_DEV,)),
            pltpu.SemaphoreType.DMA((HT_DEV,)),
        ],
        compiler_params=pltpu.CompilerParams(
            collective_id=0, has_side_effects=True, vmem_limit_bytes=60 << 20
        ),
        cost_estimate=pl.CostEstimate(
            flops=10 * 4 * ROWS * ROWS * HEAD_DIM,
            bytes_accessed=10 << 20,
            transcendentals=10 * ROWS * ROWS,
        ),
        name="attend_and_move",
    )(head_class, mask_spatial, jnp.transpose(mask_temporal, (1, 2, 0)), queries, keys, values)
    return pl.pallas_call(
        place_kernel,
        out_shape=jax.ShapeDtypeStruct((ROWS, LOCAL_HEADS * HEAD_DIM), jnp.bfloat16),
        in_specs=[smem, anywhere],
        out_specs=anywhere,
        scratch_shapes=[pltpu.SemaphoreType.DMA((LOCAL_HEADS,))],
        compiler_params=pltpu.CompilerParams(vmem_limit_bytes=8 << 20),
        name="place_heads",
    )(head_class, pltpu.with_memory_space_constraint(packed, pltpu.VMEM))


def solution(mesh):
    return jax.shard_map(
        on_device,
        mesh=mesh,
        in_specs=(
            P("seq", "head"),
            P("seq", "head"),
            P("seq", "head"),
            P("head"),
            P("seq", None, None),
            P("seq", None, None),
        ),
        out_specs=P("seq", "head"),
        check_vma=False,
    )
```

```python
import functools
import math

import jax
import jax.numpy as jnp
from jax import lax
from jax.experimental import pallas as pl
from jax.experimental.pallas import tpu as pltpu
from jax.sharding import PartitionSpec as P

HEAD_DIM = 128
TILE = 128
LOCAL_HEADS = 10
HT_DEV = 4
HS_DEV = LOCAL_HEADS - HT_DEV
ROWS = 1024
SEQ = 64
PIECE = ROWS // SEQ
NZ, NY, NC = 8, 4, 2
STEP = 256
EXP_SCALE = HEAD_DIM**-0.5 * math.log2(math.e)
NEG = -1e30
MESH = pl.DeviceIdType.MESH


def attend_rows(query, key_rows, value_rows, bias):
    scores = lax.dot_general(
        query, key_rows, (((1,), (1,)), ((), ())), preferred_element_type=jnp.float32
    )
    lows, totals = [], []
    for a in range(STEP // TILE):
        row = [
            scores[a * TILE : (a + 1) * TILE, b * TILE : (b + 1) * TILE] + bias(a, b)
            for b in range(ROWS // TILE)
        ]
        top = jnp.max(functools.reduce(jnp.maximum, row), axis=1, keepdims=True)
        weights = [jnp.exp2((part - top) * EXP_SCALE) for part in row]
        totals.append(jnp.sum(functools.reduce(jnp.add, weights), axis=1, keepdims=True))
        lows.append(jnp.concatenate([w.astype(jnp.bfloat16) for w in weights], axis=1))
    low = jnp.concatenate(lows, axis=0)
    total = jnp.concatenate(totals, axis=0)
    mixed = jnp.dot(low, value_rows, preferred_element_type=jnp.float32)
    return (mixed / total).astype(jnp.bfloat16)


def main_kernel(
    head_class_hbm, mask_s_hbm, mask_t_hbm, q_hbm, k_hbm, v_hbm, out,
    head_class, mask_s, mask_t, q_all, k_all, v_all, k_pack, v_pack, q_pack, k_got, v_got, q_got, o_send, t_bias,
    small_sem, in_sem, plane_sem, kv_send_sem, kv_recv_sem, q_send_sem, q_recv_sem, o_send_sem, o_recv_sem,
):
    me = lax.axis_index("seq")
    head = lax.axis_index("head")
    z, y, c = lax.div(me, NY * NC), lax.rem(lax.div(me, NC), NY), lax.rem(me, NC)
    z_part = [lax.rem(z + step, NZ) * (NY * NC) for step in (4, 3, 5, 2, 6, 1, 7, 0)]

    def plane(i):
        return lax.rem(y + lax.div(i, NC), NY) * NC + lax.rem(c + lax.rem(i, NC), NC)

    own_plane = [z_part[-1] + plane(i) for i in range(1, NY * NC)]
    near = [part + y * NC + c for part in z_part[:-1]] + own_plane

    def far_peers(act):
        def others(i, carry):
            rest = plane(i)
            for part in z_part[:-1]:
                act(part + rest)
            return carry

        lax.fori_loop(1, NY * NC, others, 0)

    def load(n, src, dst):
        for j in range(LOCAL_HEADS):
            cols = pl.ds(j * HEAD_DIM, HEAD_DIM)
            pltpu.make_async_copy(src.at[:, cols], dst.at[j], in_sem.at[n]).start()

    def loaded(n, dst):
        pltpu.make_async_copy(dst, dst, in_sem.at[n]).wait()

    def arrived(got, sem):
        pltpu.make_async_copy(got, got, sem).wait()

    def by_index(act):
        def one_plane(k, carry):
            for i in range(NY * NC):
                other = k * (NY * NC) + i
                pl.when(other != me)(functools.partial(act, other))
            return carry

        lax.fori_loop(0, NZ, one_plane, 0)

    def near_first(act, between=lambda: None):
        for other in near:
            act(other)
        between()
        far_peers(act)

    def send_all(src, dst, mine, send_sem, recv_sem, order=near_first):
        pltpu.make_async_copy(src(me), mine, recv_sem).start()

        def send(other):
            pltpu.make_async_remote_copy(
                src_ref=src(other),
                dst_ref=dst,
                send_sem=send_sem,
                recv_sem=recv_sem,
                device_id=(other, head),
                device_id_type=MESH,
            ).start()

        order(send)

    smalls = [
        pltpu.make_async_copy(src, dst, small_sem.at[n])
        for n, (src, dst) in enumerate(
            ((head_class_hbm, head_class), (mask_s_hbm, mask_s), (mask_t_hbm, mask_t))
        )
    ]
    smalls[0].start()
    load(1, k_hbm, k_all)

    barrier = pltpu.get_barrier_semaphore()
    for other in near:
        pl.semaphore_signal(barrier, inc=1, device_id=(other, head), device_id_type=MESH)
    for small in smalls[1:]:
        small.start()
    smalls[0].wait()

    ranks, count_t, count_s = [], jnp.int32(0), jnp.int32(HT_DEV)
    for j in range(LOCAL_HEADS):
        is_t = head_class[j] > 0
        ranks.append(jnp.where(is_t, count_t, count_s))
        count_t = count_t + jnp.where(is_t, 1, 0)
        count_s = count_s + jnp.where(is_t, 0, 1)

    def head_of(n):
        place = jnp.int32(0)
        for j, rank in enumerate(ranks):
            place = jnp.where(rank == n, j, place)
        return place

    places = [head_of(t) for t in range(HT_DEV)]

    pl.semaphore_wait(barrier, len(near))
    for other in own_plane:
        pl.semaphore_signal(plane_sem, inc=1, device_id=(other, head), device_id_type=MESH)

    loaded(1, k_all)
    for t, place in enumerate(places):
        k_pack[:, t] = k_all[place].reshape(SEQ, PIECE, HEAD_DIM)
    send_all(
        lambda s: k_pack.at[s], k_got.at[me], k_got.at[me], kv_send_sem.at[0], kv_recv_sem.at[0],
        functools.partial(
            near_first, between=lambda: pl.semaphore_wait(plane_sem, len(own_plane))
        ),
    )
    load(2, v_hbm, v_all)
    load(0, q_hbm, q_all)
    loaded(2, v_all)
    for t, place in enumerate(places):
        v_pack[:, t] = v_all[place].reshape(SEQ, PIECE, HEAD_DIM)
    send_all(
        lambda s: v_pack.at[s], v_got.at[me], v_got.at[me], kv_send_sem.at[1], kv_recv_sem.at[1]
    )
    loaded(0, q_all)
    for t, place in enumerate(places):
        q_pack[t] = q_all[place].reshape(SEQ, PIECE, HEAD_DIM)

    def send_queries(t, carry):
        send_all(
            lambda s: q_pack.at[t, s], q_got.at[t, me], q_got.at[t, me],
            q_send_sem.at[t], q_recv_sem.at[t],
        )
        return carry

    lax.fori_loop(0, HT_DEV, send_queries, 0)

    for small in smalls[1:]:
        small.wait()
    row = lax.broadcasted_iota(jnp.int32, (TILE, TILE), 0) % PIECE // 2
    col = lax.broadcasted_iota(jnp.int32, (TILE, TILE), 1) % PIECE // 2
    bias = jnp.full((TILE, TILE), NEG, jnp.float32)
    for g in range(mask_t.shape[2]):
        for i in range(2):
            for j in range(2):
                value = jnp.where(mask_t[i, j, g] > 0, 0.0, NEG).astype(jnp.float32)
                bias = jnp.where((row == 2 * g + i) & (col == 2 * g + j), value, bias)
    t_bias[...] = bias

    def spatial_head(n, carry):
        place = head_of(HT_DEV + n)

        def block(r, inner):
            at = pl.multiple_of(r * STEP, STEP)

            def tile_bias(a, b):
                allowed = mask_s[0, r * (STEP // TILE) + a, b] > 0
                return jnp.where(allowed, 0.0, NEG).astype(jnp.float32)

            out[HT_DEV + n, pl.ds(at, STEP)] = attend_rows(
                q_all[place, pl.ds(at, STEP)], k_all[place], v_all[place], tile_bias
            )
            return inner

        lax.fori_loop(0, ROWS // STEP, block, 0)
        return carry

    lax.fori_loop(0, HS_DEV, spatial_head, 0)

    arrived(k_got, kv_recv_sem.at[0])
    arrived(v_got, kv_recv_sem.at[1])

    def temporal_head(t, carry):
        arrived(q_got.at[t], q_recv_sem.at[t])

        def block(r, inner):
            frames = STEP // PIECE
            at = pl.ds(r * frames, frames)
            mixed = attend_rows(
                q_got[t, at].reshape(STEP, HEAD_DIM),
                k_got[:, t].reshape(ROWS, HEAD_DIM),
                v_got[:, t].reshape(ROWS, HEAD_DIM),
                lambda a, b: t_bias[...],
            )
            o_send[t, at] = mixed.reshape(frames, PIECE, HEAD_DIM)
            return inner

        lax.fori_loop(0, ROWS // STEP, block, 0)
        return carry

    def return_heads(heads):
        at = pl.ds(pl.multiple_of(me * PIECE, PIECE), PIECE)
        for t in heads:
            pltpu.make_async_copy(o_send.at[t, me], out.at[t, at], o_recv_sem.at[t]).start()

        def send(other):
            for t in heads:
                pltpu.make_async_remote_copy(
                    src_ref=o_send.at[t, other],
                    dst_ref=out.at[t, at],
                    send_sem=o_send_sem.at[t],
                    recv_sem=o_recv_sem.at[t],
                    device_id=(other, head),
                    device_id_type=MESH,
                ).start()

        if len(heads) == 1:
            by_index(send)
            return
        size = NY * NC
        mixed = [k * size + i for i in range(size) for k in (2, 1)]
        for other in [*range(size), *mixed, *range(3 * size, SEQ)]:
            pl.when(other != me)(functools.partial(send, other))

    def early_head(t, carry):
        temporal_head(t, carry)
        return_heads((t,))
        return carry

    lax.fori_loop(0, HT_DEV - 2, early_head, 0)
    lax.fori_loop(HT_DEV - 2, HT_DEV, temporal_head, 0)
    return_heads((HT_DEV - 2, HT_DEV - 1))

    others = pl.ds(0, SEQ - 1)
    arrived(k_pack.at[others], kv_send_sem.at[0])
    arrived(v_pack.at[others], kv_send_sem.at[1])

    def finish(t, carry):
        arrived(q_pack.at[t, others], q_send_sem.at[t])
        arrived(o_send.at[t, others], o_send_sem.at[t])
        arrived(out.at[t], o_recv_sem.at[t])
        return carry

    lax.fori_loop(0, HT_DEV, finish, 0)


def place_kernel(head_class, packed, out, sem):
    count_t, count_s = jnp.int32(0), jnp.int32(HT_DEV)
    copies = []
    for j in range(LOCAL_HEADS):
        is_t = head_class[j] > 0
        rank = jnp.where(is_t, count_t, count_s)
        count_t = count_t + jnp.where(is_t, 1, 0)
        count_s = count_s + jnp.where(is_t, 0, 1)
        copy = pltpu.make_async_copy(
            packed.at[rank], out.at[:, pl.ds(j * HEAD_DIM, HEAD_DIM)], sem.at[j]
        )
        copy.start()
        copies.append(copy)
    for copy in copies:
        copy.wait()


def on_device(queries, keys, values, head_class, mask_spatial, mask_temporal):
    smem = pl.BlockSpec(memory_space=pltpu.SMEM)
    anywhere = pl.BlockSpec(memory_space=pl.ANY)
    whole = pltpu.VMEM((LOCAL_HEADS, ROWS, HEAD_DIM), jnp.bfloat16)
    by_device = pltpu.VMEM((SEQ, HT_DEV, PIECE, HEAD_DIM), jnp.bfloat16)
    by_head = pltpu.VMEM((HT_DEV, SEQ, PIECE, HEAD_DIM), jnp.bfloat16)
    packed = pl.pallas_call(
        main_kernel,
        out_shape=pltpu.VMEM((LOCAL_HEADS, ROWS, HEAD_DIM), jnp.bfloat16),
        in_specs=[anywhere] * 6,
        out_specs=pl.BlockSpec(memory_space=pltpu.VMEM),
        scratch_shapes=[
            pltpu.SMEM(head_class.shape, jnp.int32),
            pltpu.SMEM(mask_spatial.shape, jnp.int32),
            pltpu.SMEM(mask_temporal.shape[1:] + mask_temporal.shape[:1], jnp.int32),
            whole, whole, whole,
            by_device, by_device, by_head, by_device, by_device, by_head, by_head,
            pltpu.VMEM((TILE, TILE), jnp.float32),
            pltpu.SemaphoreType.DMA((3,)),
            pltpu.SemaphoreType.DMA((3,)),
            pltpu.SemaphoreType.REGULAR,
            pltpu.SemaphoreType.DMA((2,)),
            pltpu.SemaphoreType.DMA((2,)),
            pltpu.SemaphoreType.DMA((HT_DEV,)),
            pltpu.SemaphoreType.DMA((HT_DEV,)),
            pltpu.SemaphoreType.DMA((HT_DEV,)),
            pltpu.SemaphoreType.DMA((HT_DEV,)),
        ],
        compiler_params=pltpu.CompilerParams(
            collective_id=0, has_side_effects=True, vmem_limit_bytes=60 << 20
        ),
        cost_estimate=pl.CostEstimate(
            flops=10 * 4 * ROWS * ROWS * HEAD_DIM,
            bytes_accessed=10 << 20,
            transcendentals=10 * ROWS * ROWS,
        ),
        name="attend_and_move",
    )(head_class, mask_spatial, jnp.transpose(mask_temporal, (1, 2, 0)), queries, keys, values)
    return pl.pallas_call(
        place_kernel,
        out_shape=jax.ShapeDtypeStruct((ROWS, LOCAL_HEADS * HEAD_DIM), jnp.bfloat16),
        in_specs=[smem, anywhere],
        out_specs=anywhere,
        scratch_shapes=[pltpu.SemaphoreType.DMA((LOCAL_HEADS,))],
        compiler_params=pltpu.CompilerParams(vmem_limit_bytes=8 << 20),
        name="place_heads",
    )(head_class, pltpu.with_memory_space_constraint(packed, pltpu.VMEM))


def solution(mesh):
    return jax.shard_map(
        on_device,
        mesh=mesh,
        in_specs=(
            P("seq", "head"),
            P("seq", "head"),
            P("seq", "head"),
            P("head"),
            P("seq", None, None),
            P("seq", None, None),
        ),
        out_specs=P("seq", "head"),
        check_vma=False,
    )
```
